128 devices in a mesh: row: 4 (over z_lo, core), col: 32 (over x, z_hi, y).
Axes of the slice: x: 4, y: 4, z: 4 (z_hi: 2, z_lo: 2; z = z_hi * 2 + z_lo), core: 2. Of those that a mesh axis runs over, the one named last changes fastest.
Arguments:
- points: bfloat16 [262144, 256], P(('row', 'col')), may hold values from -6 to 6
- rotated_slot: int32 [262144], P(('row', 'col')), may hold values from 0 to 262143, as said below
- fine_attend_in: bfloat16 [2, 256, 768], replicated, may hold values from -8 to 8
- fine_attend_out: bfloat16 [2, 256, 256], replicated, may hold values from -0.375 to 0.375
- fine_gate_up: bfloat16 [2, 256, 2048], replicated, may hold values from -0.375 to 0.375
- fine_down: bfloat16 [2, 1024, 256], replicated, may hold values from -0.1875 to 0.1875
- pool_weight: bfloat16 [2048, 512], replicated, may hold values from -0.125 to 0.125
- coarse_attend_in: bfloat16 [512, 1536], replicated, may hold values from -8 to 8
- coarse_attend_out: bfloat16 [512, 512], replicated, may hold values from -0.25 to 0.25
- coarse_gate_up: bfloat16 [512, 4096], replicated, may hold values from -0.25 to 0.25
- coarse_down: bfloat16 [2048, 512], replicated, may hold values from -0.125 to 0.125
- unpool_weight: bfloat16 [512, 2048], replicated, may hold values from -0.25 to 0.25
Outputs:
- refined: bfloat16 [262144, 256], P(('row', 'col'))
The draws below stay inside these ranges and needn't reach their ends.
Inputs may be any that keep to these rules, and one draw needn't show every extreme that they name: rotated_slot is a permutation of all points; each point's rotated position lies on a device with the same col index; of the points of one device at most 1280 have rotated positions on any one device, and in every col group some device sends exactly 1280 to one device.
All inputs are finite; a program needn't handle non-finite values.
Results may differ from the reference program's by a relative error of at most 0.017.
Values may be sent and summed in bfloat16 or wider, within the bound.
No kernel may reach another device: no remote copies, remote signals or barrier semaphores. Data moves between devices by JAX's collectives and lax.ppermute only.
A program may use at most 128 MiB of HBM per device.

```python
import math
import jax
import jax.numpy as jnp
from jax import lax

D = 256
HEADS = 8
FH = 1024
CW = 512
CHEADS = 8
CH = 2048
BALL = 256
PTS_DEV = 2048
POINTS = 262144
CBALL = 2048
CAP = 1280
N_ROW = 4
N_COL = 32


def draw_attend(key, model_width, leading):
    base = jnp.clip(jax.random.normal(key, (leading, model_width, 3, model_width), jnp.float32), -4.0, 4.0) / math.sqrt(model_width)
    query_part = base[:, :, 0]
    key_part = base[:, :, 1]
    value_part = base[:, :, 2]
    return jnp.concatenate((query_part, key_part, value_part), axis=-1)


def draw_fine_attend_in(key, part):
    return draw_attend(jax.random.fold_in(key, 11), D, 2).astype(jnp.bfloat16)


def draw_coarse_attend_in(key, part):
    return draw_attend(jax.random.fold_in(key, 13), CW, 1)[0].astype(jnp.bfloat16)


def draw_rotated_slot(key, part):
    key_order, key_shift, key_source, key_target = jax.random.split(jax.random.fold_in(key, 5), 4)
    orders = jax.vmap(lambda subkey: jax.random.permutation(subkey, N_ROW))(jax.random.split(key_order, N_COL))
    shifts = jax.random.randint(key_shift, (N_COL,), 1, N_ROW)
    source_rank = jax.vmap(lambda subkey: jnp.argsort(jax.random.permutation(subkey, PTS_DEV)))(jax.random.split(key_source, N_ROW * N_COL)).reshape(N_ROW, N_COL, PTS_DEV)
    target_spots = jax.vmap(lambda subkey: jax.random.permutation(subkey, PTS_DEV))(jax.random.split(key_target, N_ROW * N_COL)).reshape(N_ROW, N_COL, PTS_DEV)
    row_index = jnp.arange(N_ROW)[:, None]
    col_index = jnp.arange(N_COL)[None, :]
    first_target = orders[col_index, row_index]
    second = orders[col_index, (row_index + shifts[None, :]) % N_ROW]
    target = jnp.where(source_rank < CAP, first_target[:, :, None], second[:, :, None])
    local_spot = target_spots[target, col_index[:, :, None], source_rank]
    return ((target * N_COL + col_index[:, :, None]) * PTS_DEV + local_spot).reshape(-1).astype(jnp.int32)


def shard_levels(key, extent, shards, smallest, largest):
    def one(dim, parts):
        draws = jax.random.uniform(jax.random.fold_in(jax.random.fold_in(key, 6), dim), (parts,), jnp.float32, smallest / len(shards), largest / len(shards))
        return jnp.repeat(jnp.exp(draws), extent[dim] // parts).reshape((-1,) + (1,) * (len(extent) - dim - 1))

    gain = one(*shards[0])
    for cut in shards[1:]:
        gain = gain * one(*cut)
    return gain


def centred(rng, extent, scale, most, cuts=(), kind=jnp.bfloat16):
    drawn = scale * jax.random.normal(rng, extent, jnp.float32)
    if cuts:
        drawn = drawn * shard_levels(rng, extent, cuts, -0.22, 0.18)
    return jnp.clip(drawn, -most, most).astype(kind)


def setup_inputs(seed: int = 0) -> dict:
    key_list = jax.random.split(jax.random.key(seed), 13)
    return {
        "points": centred(key_list[0], (POINTS, D), 1.0, 6.0, ((0, 128),)),
        "rotated_slot": draw_rotated_slot(jax.random.fold_in(key_list[12], 71), 0),
        "fine_attend_in": draw_fine_attend_in(jax.random.fold_in(key_list[12], 71), 0),
        "fine_attend_out": centred(key_list[3], (2, D, D), D ** -0.5, 0.375),
        "fine_gate_up": centred(key_list[4], (2, D, 2 * FH), D ** -0.5, 0.375),
        "fine_down": centred(key_list[5], (2, FH, D), FH ** -0.5, 0.1875),
        "pool_weight": centred(key_list[6], (8 * D, CW), (8 * D) ** -0.5, 0.125),
        "coarse_attend_in": draw_coarse_attend_in(jax.random.fold_in(key_list[12], 71), 0),
        "coarse_attend_out": centred(key_list[8], (CW, CW), CW ** -0.5, 0.25),
        "coarse_gate_up": centred(key_list[9], (CW, 2 * CH), CW ** -0.5, 0.25),
        "coarse_down": centred(key_list[10], (CH, CW), CH ** -0.5, 0.125),
        "unpool_weight": centred(key_list[11], (CW, 8 * D), CW ** -0.5, 0.25),
    }


epsilon = 1e-06

def normed(source):
    widened = source.astype(jnp.float32)
    inverse_rms = lax.rsqrt(lax.optimization_barrier(jnp.mean(widened * widened, axis=-1, keepdims=True)) + epsilon)
    return (widened * inverse_rms).astype(jnp.bfloat16)

def ball_mix(queries, pairs, head_count):
    ball_count, query_len, model_width = queries.shape
    key_len = pairs.shape[1]
    head_size = model_width // head_count
    query_heads = queries.reshape(ball_count, query_len, head_count, head_size).astype(jnp.float32)
    key_heads = pairs[:, :, :model_width].reshape(ball_count, key_len, head_count, head_size).astype(jnp.float32)
    value_heads = pairs[:, :, model_width:].reshape(ball_count, key_len, head_count, head_size).astype(jnp.float32)
    scores = jnp.einsum('bqhd,bkhd->bhqk', query_heads, key_heads) * head_size ** (-0.5)
    row_max = lax.optimization_barrier(jnp.max(scores, axis=-1, keepdims=True))
    weights = jnp.exp(scores - row_max)
    weights = (weights / lax.optimization_barrier(jnp.sum(weights, axis=-1, keepdims=True))).astype(jnp.bfloat16)
    weights = lax.optimization_barrier(weights).astype(jnp.float32)
    mixture = jnp.einsum('bhqk,bkhd->bqhd', weights, value_heads)
    return mixture.reshape(ball_count, query_len, model_width).astype(jnp.bfloat16)

def attend(stream, attend_in, attend_out, head_count, ball_size):
    model_width = stream.shape[1]
    packed = jnp.dot(normed(stream), attend_in, preferred_element_type=jnp.float32).astype(jnp.bfloat16)
    queries = packed[:, :model_width].reshape(-1, ball_size, model_width)
    pairs = packed[:, model_width:].reshape(-1, ball_size, 2 * model_width)
    mixture = ball_mix(queries, pairs, head_count).reshape(-1, model_width)
    return jnp.dot(mixture, attend_out, preferred_element_type=jnp.float32)

def feed_forward(stream, gate_up, down_weight):
    both = jnp.dot(normed(stream), gate_up, preferred_element_type=jnp.float32)
    half_width = both.shape[1] // 2
    hidden = (jax.nn.silu(both[:, :half_width]) * both[:, half_width:]).astype(jnp.bfloat16)
    return (stream.astype(jnp.float32) + jnp.dot(hidden, down_weight, preferred_element_type=jnp.float32)).astype(jnp.bfloat16)

def blocked(function, source, block_size):
    pieces = source.reshape(-1, block_size, source.shape[-1])
    result = lax.map(function, pieces)
    return result.reshape(-1, result.shape[-1])

def reference(points, rotated_slot, fine_attend_in, fine_attend_out, fine_gate_up, fine_down, pool_weight, coarse_attend_in, coarse_attend_out, coarse_gate_up, coarse_down, unpool_weight):
    block_size = math.gcd(POINTS, 8192)

    def layer_one(stream):
        mixed = (stream.astype(jnp.float32) + attend(stream, fine_attend_in[0], fine_attend_out[0], HEADS, BALL)).astype(jnp.bfloat16)
        return feed_forward(mixed, fine_gate_up[0], fine_down[0])
    first = blocked(layer_one, points, block_size)
    rotated = jnp.zeros_like(first).at[rotated_slot].set(first)

    def turn(stream):
        return attend(stream, fine_attend_in[1], fine_attend_out[1], HEADS, BALL).astype(jnp.bfloat16)
    turned = blocked(turn, rotated, block_size)
    mixed_two = (first.astype(jnp.float32) + turned[rotated_slot].astype(jnp.float32)).astype(jnp.bfloat16)

    def layer_two(stream):
        return feed_forward(stream, fine_gate_up[1], fine_down[1])
    second = blocked(layer_two, mixed_two, block_size)
    pooled = jnp.dot(second.reshape(-1, 8 * D), pool_weight, preferred_element_type=jnp.float32).astype(jnp.bfloat16)

    def coarse_layer(stream):
        mixed = (stream.astype(jnp.float32) + attend(stream, coarse_attend_in, coarse_attend_out, CHEADS, CBALL)).astype(jnp.bfloat16)
        return feed_forward(mixed, coarse_gate_up, coarse_down)
    coarse = blocked(coarse_layer, pooled, CBALL)
    lifted = jnp.dot(normed(coarse), unpool_weight, preferred_element_type=jnp.float32).reshape(-1, D)
    return (second.astype(jnp.float32) + lifted).astype(jnp.bfloat16)
```

```python
import functools
import math

import jax
import jax.numpy as jnp
from jax import lax
from jax.experimental import pallas as pl
from jax.experimental.pallas import tpu as pltpu
from jax.sharding import Mesh
from jax.sharding import PartitionSpec as P

HEADS = 8
CHEADS = 8
BALL = 256
CHILDREN = 8
LANES = 128
EPSILON = 1e-06
LOG2E = 1.4426950408889634
AXES = ("z", "c", "x", "w", "y")
FIRST_CHUNKS = (2, 3, 3)
TURN_CHUNKS = (2, 3, 3)

f32 = jnp.float32
bf16 = jnp.bfloat16
LANES_BOTH = (((1,), (1,)), ((), ()))


def dot(a, b):
    return jnp.dot(a, b, preferred_element_type=f32)


def normed(wide):
    return (wide * lax.rsqrt(jnp.mean(wide * wide, axis=-1, keepdims=True) + EPSILON)).astype(bf16)


def gated(gate, up):
    half = 0.5 * gate
    return (half * up * (1.0 + jnp.tanh(half))).astype(bf16)


def masked_heads(value, heads):
    width = value.shape[1]
    lane = lax.broadcasted_iota(jnp.int32, (1, width), 1) // (width // heads)
    return [(lane == h, jnp.where(lane == h, value, jnp.zeros_like(value))) for h in range(heads)]


def ball_attend(wide, w_in, w_out):
    width = wide.shape[1]
    packed = dot(normed(wide), w_in)
    scale = LOG2E / math.sqrt(width // HEADS)
    queries = (packed[:, :width] * scale).astype(bf16)
    keys = packed[:, width : 2 * width].astype(bf16)
    values = packed[:, 2 * width :].astype(bf16)
    weights, shares, inverse = [], [], None
    for (mask, query), (_, value) in zip(
        masked_heads(queries, HEADS), masked_heads(values, HEADS)
    ):
        scores = lax.dot_general(query, keys, LANES_BOTH, preferred_element_type=f32)
        scores = jnp.exp2(scores - jnp.max(scores, axis=-1, keepdims=True))
        total = 1.0 / jnp.sum(scores, axis=-1, keepdims=True)
        if inverse is None:
            inverse = jnp.broadcast_to(total, wide.shape)
        else:
            inverse = jnp.where(mask, total, inverse)
        weights.append(scores.astype(bf16))
        shares.append(value)
    mixture = dot(jnp.concatenate(weights, 1), jnp.concatenate(shares, 0)) * inverse
    return dot(mixture.astype(bf16), w_out)


def feed_forward(stream, gate_up, down):
    wide = stream.astype(f32)
    half = down.shape[0]
    source = normed(wide)
    hidden = gated(dot(source, gate_up[:, :half]), dot(source, gate_up[:, half:]))
    return wide + dot(hidden, down[...])


def first_kernel(points, w_in, w_out, gate_up, down, out):
    for i in range(points.shape[0] // BALL):
        rows = slice(i * BALL, (i + 1) * BALL)
        wide = points[rows, :].astype(f32)
        mixed = (wide + ball_attend(wide, w_in[0], w_out[0])).astype(bf16)
        out[rows, :] = feed_forward(mixed, gate_up[0], down[0]).astype(bf16)


def picked_rows(slots, source, first_slot):
    want = lax.broadcasted_iota(jnp.int32, (BALL, 1), 0) + first_slot
    hot = jnp.where(want == slots, 1.0, 0.0).astype(bf16)
    return dot(hot, source)


def column(slots):
    tall = jnp.broadcast_to(slots.astype(f32), (8, slots.shape[1])).T
    return tall[:, :1].astype(jnp.int32)


def returned_rows(want, source, first_slot):
    have = lax.broadcasted_iota(jnp.int32, (1, source.shape[0]), 1) + first_slot
    hot = jnp.where(want == have, 1.0, 0.0).astype(bf16)
    return dot(hot, source)


def gather_rotated_kernel(spans, *refs):
    count = len(spans)
    slots, sources, acc, out = refs[:4], refs[4 : 4 + count], refs[4 + count : -1], refs[-1]
    first_slot = pl.program_id(0) * BALL
    total = acc[0][...].astype(f32) if acc else None
    for (block, start, rows), source in zip(spans, sources):
        part = picked_rows(slots[block][:, start : start + rows], source[...], first_slot)
        total = part if total is None else total + part
    out[...] = total.astype(bf16)


def turn_kernel(spans, balls_before, *refs):
    count = len(spans)
    slots, sources = refs[:4], refs[4 : 4 + count]
    acc, w_in, w_out, out = refs[4 + count :]
    first_slot = (pl.program_id(0) + balls_before) * BALL
    total = acc[...].astype(f32)
    for (block, start, rows), source in zip(spans, sources):
        total += picked_rows(slots[block][:, start : start + rows], source[...], first_slot)
    out[...] = ball_attend(total, w_in[0], w_out[0]).astype(bf16)


def gather_returned_kernel(spans, bases, slots, *refs):
    count = len(spans)
    sources, acc, out = refs[:count], refs[count:-1], refs[-1]
    want = column(slots[0])
    total = acc[0][...].astype(f32) if acc else None
    for (block, start, rows), source in zip(spans, sources):
        part = returned_rows(want, source[...], bases[block] + start)
        total = part if total is None else total + part
    out[...] = total.astype(bf16)


def second_kernel(spans, bases, slots, *refs):
    count = len(spans)
    sources = refs[:count]
    acc, first, gate_up, down, pool_weight, second, pooled, pooled_normed = refs[count:-2]
    tall = refs[-2:]
    step = pl.program_id(0)
    want = column(slots[0])
    returned = acc[...].astype(f32)
    for (block, start, rows), source in zip(spans, sources):
        returned += returned_rows(want, source[...], bases[block] + start)
    mixed = (first[...].astype(f32) + returned).astype(bf16)
    result = feed_forward(mixed, gate_up[0], down[0]).astype(bf16)
    second[...] = result
    here = pl.ds(pl.multiple_of(step * BALL, BALL), BALL)
    for half, ref in enumerate(tall):
        ref[here, :] = result[:, half * LANES : (half + 1) * LANES].astype(f32)

    @pl.when(step == pl.num_programs(0) - 1)
    def _():
        width = result.shape[1]
        count = pooled.shape[0]
        total = None
        for j in range(CHILDREN):
            child = jnp.concatenate(
                [ref[pl.ds(j, count, stride=CHILDREN), :].astype(bf16) for ref in tall], 1
            )
            part = dot(child, pool_weight[j * width : (j + 1) * width, :])
            total = part if total is None else total + part
        rounded = total.astype(bf16)
        pooled[...] = rounded
        pooled_normed[...] = normed(rounded.astype(f32))


def coarse_kernel(blocks, *refs):
    sources = refs[:blocks]
    pooled, second, w_in, w_out, gate_up, down, unpool, out, keys, values = refs[blocks:-2]
    tall = refs[-2:]
    width = pooled.shape[1]
    scale = LOG2E / math.sqrt(width // CHEADS)
    queries = (dot(sources[0][...], w_in[:, :width]) * scale).astype(bf16)
    at = 0
    for source in sources:
        rows = source.shape[0]
        keys[at : at + rows, :] = dot(source[...], w_in[:, width : 2 * width]).astype(bf16)
        values[at : at + rows, :] = dot(source[...], w_in[:, 2 * width :]).astype(bf16)
        at += rows
    halves = []
    part = width // 2
    for half in range(2):
        cols = slice(half * part, (half + 1) * part)
        mixture = None
        for mask, query in masked_heads(queries[:, cols], CHEADS // 2):
            scores = lax.dot_general(query, keys[:, cols], LANES_BOTH, preferred_element_type=f32)
            scores = jnp.exp2(scores - jnp.max(scores, axis=-1, keepdims=True))
            total = 1.0 / jnp.sum(scores, axis=-1, keepdims=True)
            mixed = dot(scores.astype(bf16), values[:, cols]) * total
            mixture = mixed if mixture is None else jnp.where(mask, mixed, mixture)
        halves.append(mixture.astype(bf16))
    mixture = jnp.concatenate(halves, 1)
    stream = (pooled[...].astype(f32) + dot(mixture, w_out[...])).astype(bf16)
    coarse = feed_forward(stream, gate_up, down).astype(bf16)
    source = normed(coarse.astype(f32))
    count, fine = source.shape[0], second.shape[1]
    for j in range(CHILDREN):
        lifted = dot(source, unpool[:, j * fine : (j + 1) * fine])
        for half, ref in enumerate(tall):
            lanes = slice(half * LANES, (half + 1) * LANES)
            ref[pl.ds(j, count, stride=CHILDREN), :] = lifted[:, lanes]
    for half, ref in enumerate(tall):
        lanes = slice(half * LANES, (half + 1) * LANES)
        out[:, lanes] = (second[:, lanes].astype(f32) + ref[...]).astype(bf16)


def whole(shape):
    return pl.BlockSpec(shape, lambda *_: (0,) * len(shape))


def layer(shape, index):
    return pl.BlockSpec((1,) + shape[1:], lambda *_: (index, 0, 0))


def ball_rows(width, before=0):
    return pl.BlockSpec((BALL, width), lambda i: (i + before, 0))


def params(mib=40):
    return pltpu.CompilerParams(vmem_limit_bytes=mib << 20)


def cost(gflop, mbyte):
    return pl.CostEstimate(
        flops=int(gflop * 1e9), bytes_accessed=int(mbyte * 1e6), transcendentals=0
    )


def swap(value, axis):
    return lax.ppermute(value, axis, [(0, 1), (1, 0)])


def turn_y(value, distance):
    size = lax.axis_size("y")
    return lax.ppermute(value, "y", [(i, (i + distance) % size) for i in range(size)])


def spread(chunks):
    z = [swap(chunk, "z") for chunk in chunks]
    sibling = [swap(chunk, "c") for chunk in chunks]
    far = [swap(chunk, "c") for chunk in z]
    return [chunks, sibling, z, far]


def spans_of(blocks, counts, wanted):
    spans, arrays = [], []
    for block, chunk in wanted:
        start = sum(counts[:chunk]) * BALL
        spans.append((block, start, counts[chunk] * BALL))
        arrays.append(blocks[block][chunk])
    return tuple(spans), arrays


def local(
    points,
    rotated_slot,
    fine_attend_in,
    fine_attend_out,
    fine_gate_up,
    fine_down,
    pool_weight,
    coarse_attend_in,
    coarse_attend_out,
    coarse_gate_up,
    coarse_down,
    unpool_weight,
):
    rows, width = points.shape
    balls = rows // BALL
    cols = lax.axis_size("x") * lax.axis_size("w") * lax.axis_size("y")
    mine = lax.axis_index("z") * 2 + lax.axis_index("c")
    col = lax.axis_index(("x", "w", "y"))

    own_slot = rotated_slot.reshape(1, rows)
    z_slot = swap(own_slot, "z")
    group_slots = [own_slot, swap(own_slot, "c"), z_slot, swap(z_slot, "c")]
    my_base = (mine * cols + col) * rows
    relative = [slot - my_base for slot in group_slots]
    bases = jnp.stack([((mine ^ flip) * cols + col) * rows for flip in (0, 1, 2, 3)]).astype(
        jnp.int32
    )
    own_balls = rotated_slot.reshape(balls, 1, BALL)

    first_chunks, before = [], 0
    for count in FIRST_CHUNKS:
        first_chunks.append(
            pl.pallas_call(
                first_kernel,
                grid=(count,),
                in_specs=[
                    ball_rows(width, before),
                    layer(fine_attend_in.shape, 0),
                    layer(fine_attend_out.shape, 0),
                    layer(fine_gate_up.shape, 0),
                    layer(fine_down.shape, 0),
                ],
                out_specs=ball_rows(width),
                out_shape=jax.ShapeDtypeStruct((count * BALL, width), bf16),
                compiler_params=params(),
                cost_estimate=cost(1.2 * count, 0.5),
            )(points, fine_attend_in, fine_attend_out, fine_gate_up, fine_down)
        )
        before += count

    blocks = spread(first_chunks)
    last = len(FIRST_CHUNKS) - 1

    def gather_rotated(wanted, acc):
        spans, arrays = spans_of(blocks, FIRST_CHUNKS, wanted)
        extra = [] if acc is None else [acc]
        return pl.pallas_call(
            functools.partial(gather_rotated_kernel, spans),
            grid=(balls,),
            in_specs=[whole((1, rows))] * 4
            + [whole(array.shape) for array in arrays]
            + [ball_rows(width)] * len(extra),
            out_specs=ball_rows(width),
            out_shape=jax.ShapeDtypeStruct((rows, width), bf16),
            compiler_params=params(),
            cost_estimate=cost(1.3 * len(wanted), 2),
        )(*relative, *arrays, *extra)

    acc = gather_rotated([(b, c) for b in (0, 1) for c in range(last + 1)], None)
    for chunk in range(last):
        acc = gather_rotated([(2, chunk), (3, chunk)], acc)
    spans, arrays = spans_of(blocks, FIRST_CHUNKS, [(2, last), (3, last)])
    turned_chunks, before = [], 0
    for count in TURN_CHUNKS:
        turned_chunks.append(
            pl.pallas_call(
                functools.partial(turn_kernel, spans, before),
                grid=(count,),
                in_specs=[whole((1, rows))] * 4
                + [whole(array.shape) for array in arrays]
                + [
                    ball_rows(width, before),
                    layer(fine_attend_in.shape, 1),
                    layer(fine_attend_out.shape, 1),
                ],
                out_specs=ball_rows(width),
                out_shape=jax.ShapeDtypeStruct((count * BALL, width), bf16),
                compiler_params=params(),
                cost_estimate=cost(1.2 * count, 0.5),
            )(*relative, *arrays, acc, fine_attend_in, fine_attend_out)
        )
        before += count

    back = spread(turned_chunks)
    last = len(TURN_CHUNKS) - 1
    smem = pl.BlockSpec(memory_space=pltpu.SMEM)
    slot_spec = pl.BlockSpec((1, 1, BALL), lambda i: (i, 0, 0))

    def gather_returned(wanted, acc):
        spans, arrays = spans_of(back, TURN_CHUNKS, wanted)
        extra = [] if acc is None else [acc]
        return pl.pallas_call(
            functools.partial(gather_returned_kernel, spans),
            grid=(balls,),
            in_specs=[smem, slot_spec]
            + [whole(array.shape) for array in arrays]
            + [ball_rows(width)] * len(extra),
            out_specs=ball_rows(width),
            out_shape=jax.ShapeDtypeStruct((rows, width), bf16),
            compiler_params=params(),
            cost_estimate=cost(1.3 * len(wanted), 2),
        )(bases, own_balls, *arrays, *extra)

    acc = gather_returned([(b, c) for b in (0, 1) for c in range(last + 1)], None)
    for chunk in range(last):
        acc = gather_returned([(2, chunk), (3, chunk)], acc)
    spans, arrays = spans_of(back, TURN_CHUNKS, [(2, last), (3, last)])
    first = jnp.concatenate(first_chunks, 0)
    pooled_rows, coarse_width = rows // CHILDREN, pool_weight.shape[1]
    second, pooled, pooled_normed = pl.pallas_call(
        functools.partial(second_kernel, spans),
        grid=(balls,),
        in_specs=[smem, slot_spec]
        + [whole(array.shape) for array in arrays]
        + [
            ball_rows(width),
            ball_rows(width),
            layer(fine_gate_up.shape, 1),
            layer(fine_down.shape, 1),
            whole(pool_weight.shape),
        ],
        out_specs=[
            ball_rows(width),
            whole((pooled_rows, coarse_width)),
            whole((pooled_rows, coarse_width)),
        ],
        out_shape=[
            jax.ShapeDtypeStruct((rows, width), bf16),
            jax.ShapeDtypeStruct((pooled_rows, coarse_width), bf16),
            jax.ShapeDtypeStruct((pooled_rows, coarse_width), bf16),
        ],
        scratch_shapes=[pltpu.VMEM((rows, LANES), f32)] * 2,
        compiler_params=params(),
        cost_estimate=cost(8, 4),
    )(bases, own_balls, *arrays, acc, first, fine_gate_up, fine_down, pool_weight)

    other = swap(pooled_normed, "w")
    opposite = turn_y(pooled_normed, 2)
    gathered = [
        pooled_normed,
        other,
        turn_y(pooled_normed, 1),
        turn_y(pooled_normed, -1),
        opposite,
        turn_y(other, 1),
        turn_y(other, -1),
        swap(opposite, "w"),
    ]
    operands = [
        pooled,
        second,
        coarse_attend_in,
        coarse_attend_out,
        coarse_gate_up,
        coarse_down,
        unpool_weight,
    ]
    return pl.pallas_call(
        functools.partial(coarse_kernel, len(gathered)),
        grid=(1,),
        in_specs=[whole(array.shape) for array in gathered + operands],
        out_specs=whole((rows, width)),
        out_shape=jax.ShapeDtypeStruct((rows, width), bf16),
        scratch_shapes=[
            pltpu.VMEM((pooled_rows * len(gathered), coarse_width), bf16),
            pltpu.VMEM((pooled_rows * len(gathered), coarse_width), bf16),
            pltpu.VMEM((rows, LANES), f32),
            pltpu.VMEM((rows, LANES), f32),
        ],
        compiler_params=params(56),
        cost_estimate=cost(10, 16),
    )(*gathered, *operands)


def solution(mesh):
    torus = Mesh(mesh.devices.reshape(2, 2, 4, 2, 4), AXES)
    split = P(AXES, None)
    return jax.shard_map(
        local,
        mesh=torus,
        in_specs=(split, P(AXES)) + (P(),) * 10,
        out_specs=split,
        check_vma=False,
    )
```

```python
import functools
import math

import jax
import jax.numpy as jnp
from jax import lax
from jax.experimental import pallas as pl
from jax.experimental.pallas import tpu as pltpu
from jax.sharding import Mesh
from jax.sharding import PartitionSpec as P

HEADS = 8
CHEADS = 8
BALL = 256
CHILDREN = 8
LANES = 128
EPSILON = 1e-06
LOG2E = 1.4426950408889634
AXES = ("z", "c", "x", "w", "y")
FIRST_CHUNKS = (2, 4, 2)
TURN_CHUNKS = (2, 4, 2)

f32 = jnp.float32
bf16 = jnp.bfloat16
LANES_BOTH = (((1,), (1,)), ((), ()))


def dot(a, b):
    return jnp.dot(a, b, preferred_element_type=f32)


def normed(wide):
    return (wide * lax.rsqrt(jnp.mean(wide * wide, axis=-1, keepdims=True) + EPSILON)).astype(bf16)


def gated(gate, up):
    half = 0.5 * gate
    return (half * up * (1.0 + jnp.tanh(half))).astype(bf16)


def masked_heads(value, heads):
    width = value.shape[1]
    lane = lax.broadcasted_iota(jnp.int32, (1, width), 1) // (width // heads)
    return [(lane == h, jnp.where(lane == h, value, jnp.zeros_like(value))) for h in range(heads)]


def ball_attend(wide, w_in, w_out):
    width = wide.shape[1]
    packed = dot(normed(wide), w_in)
    scale = LOG2E / math.sqrt(width // HEADS)
    queries = (packed[:, :width] * scale).astype(bf16)
    keys = packed[:, width : 2 * width].astype(bf16)
    values = packed[:, 2 * width :].astype(bf16)
    weights, shares, inverse = [], [], None
    for (mask, query), (_, value) in zip(
        masked_heads(queries, HEADS), masked_heads(values, HEADS)
    ):
        scores = lax.dot_general(query, keys, LANES_BOTH, preferred_element_type=f32)
        scores = jnp.exp2(scores - jnp.max(scores, axis=-1, keepdims=True))
        total = 1.0 / jnp.sum(scores, axis=-1, keepdims=True)
        if inverse is None:
            inverse = jnp.broadcast_to(total, wide.shape)
        else:
            inverse = jnp.where(mask, total, inverse)
        weights.append(scores.astype(bf16))
        shares.append(value)
    mixture = dot(jnp.concatenate(weights, 1), jnp.concatenate(shares, 0)) * inverse
    return dot(mixture.astype(bf16), w_out)


def feed_forward(stream, gate_up, down):
    wide = stream.astype(f32)
    half = down.shape[0]
    source = normed(wide)
    hidden = gated(dot(source, gate_up[:, :half]), dot(source, gate_up[:, half:]))
    return wide + dot(hidden, down[...])


def first_kernel(before, points, w_in, w_out, gate_up, down, *refs):
    out, held, sems = refs[-7], refs[-6:-1], refs[-1]
    sources = (
        points.at[pl.ds(before * BALL, out.shape[0]), :],
        *(ref.at[pl.ds(0, 1)] for ref in (w_in, w_out, gate_up, down)),
    )
    copies = [
        pltpu.make_async_copy(source, ref, sems.at[i])
        for i, (source, ref) in enumerate(zip(sources, held))
    ]
    for copy in copies:
        copy.start()
    for copy in copies[:3]:
        copy.wait()
    rows, w_in, w_out, gate_up, down = held
    for pair in range(0, out.shape[0], 2 * BALL):
        mixed = []
        for at in range(pair, pair + 2 * BALL, BALL):
            wide = rows[at : at + BALL, :].astype(f32)
            mixed.append((wide + ball_attend(wide, w_in[0], w_out[0])).astype(bf16))
        if pair == 0:
            for copy in copies[3:]:
                copy.wait()
        result = feed_forward(jnp.concatenate(mixed, 0), gate_up.at[0], down.at[0])
        out[pair : pair + 2 * BALL, :] = result.astype(bf16)


def picked_rows(slots, source, first_slot):
    want = lax.broadcasted_iota(jnp.int32, (BALL, 1), 0) + first_slot
    hot = jnp.where(want == slots, 1.0, 0.0).astype(bf16)
    return dot(hot, source)


def returned_rows(want, source, first_slot):
    hot = [
        jnp.where(want == first_slot + at, 1.0, 0.0).astype(bf16)
        for at in range(0, source.shape[0], LANES)
    ]
    return dot(jnp.concatenate(hot, 1), source)


def gather_rotated_kernel(spans, bases, *refs):
    count = len(spans)
    slots, sources, acc, out = refs[:4], refs[4 : 4 + count], refs[4 + count : -1], refs[-1]
    for i in range(2):
        here = slice(i * BALL, (i + 1) * BALL)
        first_slot = (2 * pl.program_id(0) + i) * BALL + bases[0]
        total = acc[0][here, :].astype(f32) if acc else None
        for (block, start, rows), source in zip(spans, sources):
            part = picked_rows(slots[block][:, start : start + rows], source[...], first_slot)
            total = part if total is None else total + part
        out[here, :] = total.astype(bf16)


def turn_kernel(spans, balls_before, bases, *refs):
    count = len(spans)
    slots, sources = refs[:4], refs[4 : 4 + count]
    acc, w_in, w_out = refs[4 + count : 7 + count]
    out = refs[-1]
    for i in range(acc.shape[0] // BALL):
        here = slice(i * BALL, (i + 1) * BALL)
        first_slot = (2 * pl.program_id(0) + i + balls_before) * BALL + bases[0]
        total = acc[here, :].astype(f32)
        for (block, start, rows), source in zip(spans, sources):
            total += picked_rows(slots[block][:, start : start + rows], source[...], first_slot)
        out[here, :] = ball_attend(total, w_in[0], w_out[0]).astype(bf16)


def columns_kernel(slots, out):
    tall = jnp.broadcast_to(slots[0].astype(f32), (LANES, BALL)).T
    out[...] = tall.astype(jnp.int32) - lax.broadcasted_iota(jnp.int32, (BALL, LANES), 1)


def gather_returned_kernel(spans, bases, wanted, *refs):
    count = len(spans)
    sources, acc, out = refs[:count], refs[count:-1], refs[-1]
    want = wanted[...]
    total = acc[0][...].astype(f32) if acc else None
    for (block, start, rows), source in zip(spans, sources):
        part = returned_rows(want, source[...], bases[block] + start)
        total = part if total is None else total + part
    out[...] = total.astype(bf16)


def second_kernel(spans, bases, wanted, *refs):
    count = len(spans)
    sources = refs[:count]
    acc, first_a, first_b, first_c, gate_up, down, pool_weight = refs[count : count + 7]
    second, pooled, pooled_normed = refs[count + 7 : -2]
    tall = refs[-2:]
    step = pl.program_id(0)
    want = wanted[...]
    returned = acc[...].astype(f32)
    for (block, start, rows), source in zip(spans, sources):
        returned += returned_rows(want, source[...], bases[block] + start)
    inner = jnp.where(step == 0, first_a[...], first_b[...])
    first = jnp.where(step == pl.num_programs(0) - 1, first_c[...], inner)
    mixed = (first.astype(f32) + returned).astype(bf16)
    result = feed_forward(mixed, gate_up.at[0], down.at[0]).astype(bf16)
    second[...] = result
    size = acc.shape[0]
    here = pl.ds(pl.multiple_of(step * size, size), size)
    for half, ref in enumerate(tall):
        ref[here, :] = result[:, half * LANES : (half + 1) * LANES].astype(f32)

    @pl.when(step == pl.num_programs(0) - 1)
    def _():
        width = result.shape[1]
        count = pooled.shape[0]
        total = None
        for j in range(CHILDREN):
            child = jnp.concatenate(
                [ref[pl.ds(j, count, stride=CHILDREN), :].astype(bf16) for ref in tall], 1
            )
            part = dot(child, pool_weight[j * width : (j + 1) * width, :])
            total = part if total is None else total + part
        rounded = total.astype(bf16)
        pooled[...] = rounded
        pooled_normed[...] = normed(rounded.astype(f32))


def coarse_share(queries, sources, w_in, keys, values):
    width = queries.shape[1]
    at = 0
    for source in sources:
        rows = source.shape[0]
        pair = dot(source[...], w_in[:, width:])
        keys[at : at + rows, :] = pair[:, :width].astype(bf16)
        values[at : at + rows, :] = pair[:, width:].astype(bf16)
        at += rows
    part = width // 2
    shares = []
    for half in range(2):
        cols = slice(half * part, (half + 1) * part)
        share = None
        for mask, query in masked_heads(queries[:, cols], CHEADS // 2):
            scores = lax.dot_general(query, keys[:at, cols], LANES_BOTH, preferred_element_type=f32)
            most = jnp.max(scores, axis=-1, keepdims=True)
            scores = jnp.exp2(scores - most)
            total = jnp.sum(scores, axis=-1, keepdims=True)
            mixed = dot(scores.astype(bf16), values[:at, cols])
            if share is None:
                share = [mixed] + [jnp.broadcast_to(x, mixed.shape) for x in (most, total)]
            else:
                share = [jnp.where(mask, x, old) for x, old in zip((mixed, most, total), share)]
        shares.append(share)
    return [jnp.concatenate(pair, 1) for pair in zip(*shares)]


def coarse_early_kernel(blocks, *refs):
    sources = refs[:blocks]
    w_in, out_queries, mixture, most, total, keys, values = refs[blocks:]
    width = out_queries.shape[1]
    scale = LOG2E / math.sqrt(width // CHEADS)
    queries = (dot(sources[0][...], w_in[:, :width]) * scale).astype(bf16)
    out_queries[...] = queries
    mixture[...], most[...], total[...] = coarse_share(queries, sources, w_in, keys, values)


def coarse_kernel(blocks, *refs):
    sources, early = refs[:blocks], refs[blocks : blocks + 4]
    pooled, second, w_in, w_out, gate_up, down, unpool, out, keys, values = refs[blocks + 4 : -2]
    tall = refs[-2:]
    mixed_late, most_late, total_late = coarse_share(early[0][...], sources, w_in, keys, values)
    mixed, most, total = (ref[...] for ref in early[1:])
    top = jnp.maximum(most, most_late)
    keep, keep_late = jnp.exp2(most - top), jnp.exp2(most_late - top)
    mixture = (mixed * keep + mixed_late * keep_late) / (total * keep + total_late * keep_late)
    stream = (pooled[...].astype(f32) + dot(mixture.astype(bf16), w_out[...])).astype(bf16)
    coarse = feed_forward(stream, gate_up, down).astype(bf16)
    source = normed(coarse.astype(f32))
    count, fine = source.shape[0], second.shape[1]
    for j in range(CHILDREN):
        lifted = dot(source, unpool[:, j * fine : (j + 1) * fine])
        for half, ref in enumerate(tall):
            lanes = slice(half * LANES, (half + 1) * LANES)
            ref[pl.ds(j, count, stride=CHILDREN), :] = lifted[:, lanes]
    for half, ref in enumerate(tall):
        lanes = slice(half * LANES, (half + 1) * LANES)
        out[:, lanes] = (second[:, lanes].astype(f32) + ref[...]).astype(bf16)


def whole(shape):
    return pl.BlockSpec(shape, lambda *_: (0,) * len(shape))


def layer(shape, index):
    return pl.BlockSpec((1,) + shape[1:], lambda *_: (index, 0, 0))


def ball_rows(width, before=0):
    return pl.BlockSpec((BALL, width), lambda i: (i + before, 0))


def params(mib=20):
    return pltpu.CompilerParams(vmem_limit_bytes=mib << 20)


def cost(gflop, mbyte):
    return pl.CostEstimate(
        flops=int(gflop * 1e9), bytes_accessed=int(mbyte * 1e6), transcendentals=0
    )


def swap(value, axis):
    return lax.ppermute(value, axis, [(0, 1), (1, 0)])


def turn_y(value, distance):
    size = lax.axis_size("y")
    return lax.ppermute(value, "y", [(i, (i + distance) % size) for i in range(size)])


def after(value, *others):
    if not others:
        return value
    return lax.optimization_barrier((value, *others))[0]


def spread(chunks, z):
    late = [after(chunk, chunks[-1]) for chunk in chunks[:-1]] + [chunks[-1]]
    sibling = [swap(chunk, "c") for chunk in late]
    far = [swap(chunk, "c") for chunk in z[:-1]]
    return [chunks, sibling, z, far]


def spans_of(blocks, counts, wanted):
    spans, arrays = [], []
    for block, chunk in wanted:
        start = sum(counts[:chunk]) * BALL
        spans.append((block, start, counts[chunk] * BALL))
        arrays.append(blocks[block][chunk])
    return tuple(spans), arrays


def local(
    points,
    rotated_slot,
    fine_attend_in,
    fine_attend_out,
    fine_gate_up,
    fine_down,
    pool_weight,
    coarse_attend_in,
    coarse_attend_out,
    coarse_gate_up,
    coarse_down,
    unpool_weight,
):
    rows, width = points.shape
    balls = rows // BALL
    cols = lax.axis_size("x") * lax.axis_size("w") * lax.axis_size("y")
    mine = lax.axis_index("z") * 2 + lax.axis_index("c")
    col = lax.axis_index(("x", "w", "y"))

    own_slot = rotated_slot.reshape(1, rows)
    far_slot = lax.ppermute(own_slot, ("z", "c"), [(0, 3), (1, 2), (2, 1), (3, 0)])
    group_slots = [own_slot, swap(own_slot, "c"), swap(own_slot, "z"), far_slot]
    bases = jnp.stack([((mine ^ flip) * cols + col) * rows for flip in (0, 1, 2, 3)]).astype(
        jnp.int32
    )
    smem = pl.BlockSpec(memory_space=pltpu.SMEM)

    weights = (fine_attend_in, fine_attend_out, fine_gate_up, fine_down)
    first_chunks, arrived, before = [], [], 0
    for count in FIRST_CHUNKS:
        if first_chunks:
            pending = [first_chunks[-1]] + (group_slots[1:] if not arrived else arrived[:1])
            arrived.append(swap(after(first_chunks[-1], *arrived[-1:]), "z"))
        else:
            pending = []
        first_chunks.append(
            pl.pallas_call(
                functools.partial(first_kernel, before),
                name="first",
                in_specs=[pl.BlockSpec(memory_space=pl.ANY)] * 5,
                out_specs=pl.BlockSpec(memory_space=pltpu.VMEM),
                out_shape=jax.ShapeDtypeStruct((count * BALL, width), bf16),
                scratch_shapes=[pltpu.VMEM((count * BALL, width), bf16)]
                + [pltpu.VMEM((1,) + weight.shape[1:], bf16) for weight in weights]
                + [pltpu.SemaphoreType.DMA((5,))],
                compiler_params=params(60),
                cost_estimate=cost(1.2 * count, 0.5),
            )(after(points, *pending), *weights)
        )
        before += count
    arrived.append(swap(after(first_chunks[-1], arrived[-1]), "z"))
    blocks = spread(first_chunks, arrived)

    last = len(FIRST_CHUNKS) - 1
    wanted = pl.pallas_call(
        columns_kernel,
        name="columns",
        grid=(balls,),
        in_specs=[pl.BlockSpec((1, 1, BALL), lambda i: (i, 0, 0))],
        out_specs=ball_rows(LANES),
        out_shape=jax.ShapeDtypeStruct((rows, LANES), jnp.int32),
        compiler_params=params(),
        cost_estimate=cost(0.5, 1),
    )(after(rotated_slot, first_chunks[-1]).reshape(balls, 1, BALL))

    two_balls = pl.BlockSpec((2 * BALL, width), lambda i: (i, 0))

    def gather_rotated(picked, acc):
        spans, arrays = spans_of(blocks, FIRST_CHUNKS, picked)
        return pl.pallas_call(
            functools.partial(gather_rotated_kernel, spans),
            name="gather_rotated",
            grid=(balls // 2,),
            in_specs=[smem]
            + [whole((1, rows))] * 4
            + [whole(array.shape) for array in arrays]
            + [two_balls] * len(acc),
            out_specs=two_balls,
            out_shape=jax.ShapeDtypeStruct((rows, width), bf16),
            compiler_params=params(),
            cost_estimate=cost(7, 4),
        )(bases, *group_slots, *arrays, *acc)

    early = [(b, c) for b in (0, 1) for c in range(last + 1)]
    early += [(b, c) for c in range(last) for b in (2, 3)]
    acc = gather_rotated(early, [])
    blocks[3].append(swap(after(blocks[2][last], acc), "c"))
    spans, arrays = spans_of(blocks, FIRST_CHUNKS, [(2, last), (3, last)])
    turned_chunks, arrived, before = [], [], 0
    for count in TURN_CHUNKS:
        turned_chunks.append(
            pl.pallas_call(
                functools.partial(turn_kernel, spans, before),
                name="turn",
                grid=(count // 2,),
                in_specs=[smem]
                + [whole((1, rows))] * 4
                + [whole(array.shape) for array in arrays]
                + [
                    pl.BlockSpec((2 * BALL, width), lambda i, b=before // 2: (i + b, 0)),
                    layer(fine_attend_in.shape, 1),
                    layer(fine_attend_out.shape, 1),
                ]
                + [pl.BlockSpec(memory_space=pl.ANY)] * len(turned_chunks[-1:]),
                out_specs=pl.BlockSpec((2 * BALL, width), lambda i: (i, 0)),
                out_shape=jax.ShapeDtypeStruct((count * BALL, width), bf16),
                compiler_params=params(),
                cost_estimate=cost(1.2 * count, 0.5),
            )(
                bases,
                *group_slots,
                *arrays,
                acc,
                fine_attend_in,
                fine_attend_out,
                *turned_chunks[-1:],
            )
        )
        arrived.append(swap(after(turned_chunks[-1], *arrived[-1:]), "z"))
        before += count

    back = spread(turned_chunks, arrived)
    last = len(TURN_CHUNKS) - 1

    def gather_returned(picked, acc):
        spans, arrays = spans_of(back, TURN_CHUNKS, picked)
        return pl.pallas_call(
            functools.partial(gather_returned_kernel, spans),
            name="gather_returned",
            grid=(balls // 2,),
            in_specs=[smem, pl.BlockSpec((2 * BALL, LANES), lambda i: (i, 0))]
            + [whole(array.shape) for array in arrays]
            + [two_balls] * len(acc),
            out_specs=two_balls,
            out_shape=jax.ShapeDtypeStruct((rows, width), bf16),
            compiler_params=params(),
            cost_estimate=cost(7, 4),
        )(bases, wanted, *arrays, *acc)

    acc = gather_returned(early, [])
    back[3].append(swap(after(back[2][last], acc), "c"))
    spans, arrays = spans_of(back, TURN_CHUNKS, [(2, last), (3, last)])
    pooled_rows, coarse_width = rows // CHILDREN, pool_weight.shape[1]
    second, pooled, pooled_normed = pl.pallas_call(
        functools.partial(second_kernel, spans),
        name="second",
        grid=(balls // 2,),
        in_specs=[smem, pl.BlockSpec((2 * BALL, LANES), lambda i: (i, 0))]
        + [whole(array.shape) for array in arrays]
        + [
            two_balls,
            pl.BlockSpec((2 * BALL, width), lambda i: (0, 0)),
            pl.BlockSpec((2 * BALL, width), lambda i: (jnp.clip(i - 1, 0, 1), 0)),
            pl.BlockSpec((2 * BALL, width), lambda i: (0, 0)),
            layer(fine_gate_up.shape, 1),
            layer(fine_down.shape, 1),
            whole(pool_weight.shape),
        ],
        out_specs=[
            two_balls,
            whole((pooled_rows, coarse_width)),
            whole((pooled_rows, coarse_width)),
        ],
        out_shape=[
            jax.ShapeDtypeStruct((rows, width), bf16),
            jax.ShapeDtypeStruct((pooled_rows, coarse_width), bf16),
            jax.ShapeDtypeStruct((pooled_rows, coarse_width), bf16),
        ],
        scratch_shapes=[pltpu.VMEM((rows, LANES), f32)] * 2,
        compiler_params=params(),
        cost_estimate=cost(8, 4),
    )(bases, wanted, *arrays, acc, *first_chunks, fine_gate_up, fine_down, pool_weight)

    other = swap(pooled_normed, "w")
    opposite = turn_y(pooled_normed, 2)
    up, down_y = turn_y(pooled_normed, 1), turn_y(pooled_normed, -1)
    late = [up, down_y, turn_y(other, 1), turn_y(other, -1), swap(opposite, "w")]
    soon = [pooled_normed, other, opposite]
    square = (pooled_rows, coarse_width)
    held = [pltpu.VMEM((pooled_rows * len(late), coarse_width), bf16)] * 2
    early = pl.pallas_call(
        functools.partial(coarse_early_kernel, len(soon)),
        name="coarse_early",
        grid=(1,),
        in_specs=[whole(square)] * len(soon) + [whole(coarse_attend_in.shape)],
        out_specs=[whole(square)] * 4,
        out_shape=[jax.ShapeDtypeStruct(square, bf16)] + [jax.ShapeDtypeStruct(square, f32)] * 3,
        scratch_shapes=held,
        compiler_params=params(),
        cost_estimate=cost(5, 4),
    )(*soon, coarse_attend_in)
    operands = [
        *late,
        *early,
        pooled,
        second,
        coarse_attend_in,
        coarse_attend_out,
        coarse_gate_up,
        coarse_down,
        unpool_weight,
    ]
    return pl.pallas_call(
        functools.partial(coarse_kernel, len(late)),
        name="coarse",
        grid=(1,),
        in_specs=[whole(array.shape) for array in operands],
        out_specs=whole((rows, width)),
        out_shape=jax.ShapeDtypeStruct((rows, width), bf16),
        scratch_shapes=held + [pltpu.VMEM((rows, LANES), f32)] * 2,
        compiler_params=params(40),
        cost_estimate=cost(8, 16),
    )(*operands)


def solution(mesh):
    torus = Mesh(mesh.devices.reshape(2, 2, 4, 2, 4), AXES)
    split = P(AXES, None)
    return jax.shard_map(
        local,
        mesh=torus,
        in_specs=(split, P(AXES)) + (P(),) * 10,
        out_specs=split,
        check_vma=False,
    )
```

```python
import functools
import math

import jax
import jax.numpy as jnp
from jax import lax
from jax.experimental import pallas as pl
from jax.experimental.pallas import tpu as pltpu
from jax.sharding import Mesh
from jax.sharding import PartitionSpec as P

HEADS = 8
CHEADS = 8
BALL = 256
CHILDREN = 8
LANES = 128
EPSILON = 1e-06
LOG2E = 1.4426950408889634
AXES = ("z", "c", "x", "w", "y")
FIRST_CHUNKS = (2, 4, 2)
TURN_CHUNKS = (2, 4, 2)

f32 = jnp.float32
bf16 = jnp.bfloat16
LANES_BOTH = (((1,), (1,)), ((), ()))


def dot(a, b):
    return jnp.dot(a, b, preferred_element_type=f32)


def normed(wide):
    return (wide * lax.rsqrt(jnp.mean(wide * wide, axis=-1, keepdims=True) + EPSILON)).astype(bf16)


def gated(gate, up):
    half = 0.5 * gate
    return (half * up * (1.0 + jnp.tanh(half))).astype(bf16)


def masked_heads(value, heads):
    width = value.shape[1]
    lane = lax.broadcasted_iota(jnp.int32, (1, width), 1) // (width // heads)
    return [(lane == h, jnp.where(lane == h, value, jnp.zeros_like(value))) for h in range(heads)]


def ball_attend(wide, w_in, w_out):
    width = wide.shape[1]
    packed = dot(normed(wide), w_in)
    scale = LOG2E / math.sqrt(width // HEADS)
    queries = (packed[:, :width] * scale).astype(bf16)
    keys = packed[:, width : 2 * width].astype(bf16)
    values = packed[:, 2 * width :].astype(bf16)
    weights, shares, inverse = [], [], None
    for (mask, query), (_, value) in zip(
        masked_heads(queries, HEADS), masked_heads(values, HEADS)
    ):
        scores = lax.dot_general(query, keys, LANES_BOTH, preferred_element_type=f32)
        scores = jnp.exp2(scores - jnp.max(scores, axis=-1, keepdims=True))
        total = 1.0 / jnp.sum(scores, axis=-1, keepdims=True)
        if inverse is None:
            inverse = jnp.broadcast_to(total, wide.shape)
        else:
            inverse = jnp.where(mask, total, inverse)
        weights.append(scores.astype(bf16))
        shares.append(value)
    mixture = dot(jnp.concatenate(weights, 1), jnp.concatenate(shares, 0)) * inverse
    return dot(mixture.astype(bf16), w_out)


def feed_forward(stream, gate_up, down):
    wide = stream.astype(f32)
    half = down.shape[0]
    source = normed(wide)
    hidden = gated(dot(source, gate_up[:, :half]), dot(source, gate_up[:, half:]))
    return wide + dot(hidden, down[...])


def near_rotated(spans, bases, slots, sources, out):
    @pl.loop(0, out.shape[0] // (2 * BALL))
    def _(step):
        for i in range(2):
            ball = 2 * step + i
            total = None
            for (block, start, rows), source in zip(spans, sources):
                at = slots[block][:, start : start + rows]
                part = picked_rows(at, source[...], ball * BALL + bases[0])
                total = part if total is None else total + part
            here = pl.ds(pl.multiple_of(ball * BALL, BALL), BALL)
            out[here, :] = total.astype(bf16)


def near_returned(spans, bases, wanted, sources, out):
    @pl.loop(0, out.shape[0] // (2 * BALL))
    def _(step):
        here = pl.ds(pl.multiple_of(step * 2 * BALL, 2 * BALL), 2 * BALL)
        want, total = wanted[here, :], None
        for (block, start, rows), source in zip(spans, sources):
            part = returned_rows(want, source[...], bases[block] + start)
            total = part if total is None else total + part
        out[here, :] = total.astype(bf16)


def last_first_kernel(before, spans, bases, slot_own, slot_core, slot_z, *refs):
    count = len(spans) - 1
    own, sources = refs[:5], refs[5 : 5 + count]
    out, near, held = refs[5 + count], refs[6 + count], refs[7 + count : 7 + 2 * count]
    sems = refs[7 + 2 * count]
    copies = [
        pltpu.make_async_copy(source, ref, sems.at[i])
        for i, (source, ref) in enumerate(zip(sources, held))
    ]
    first_kernel(before, *own, out, *refs[8 + 2 * count :], extra=copies)
    near_rotated(spans, bases, (slot_own, slot_core, slot_z), (*held, out), near)


def first_kernel(before, points, w_in, w_out, gate_up, down, *refs, extra=()):
    out, held, sems = refs[-7], refs[-6:-1], refs[-1]
    sources = (
        points.at[pl.ds(before * BALL, out.shape[0]), :],
        *(ref.at[pl.ds(0, 1)] for ref in (w_in, w_out, gate_up, down)),
    )
    copies = [
        pltpu.make_async_copy(source, ref, sems.at[i])
        for i, (source, ref) in enumerate(zip(sources, held))
    ]
    for copy in copies:
        copy.start()
    for copy in extra:
        copy.start()
    for copy in copies[:3]:
        copy.wait()
    rows, w_in, w_out, gate_up, down = held
    for pair in range(0, out.shape[0], 2 * BALL):
        mixed = []
        for at in range(pair, pair + 2 * BALL, BALL):
            wide = rows[at : at + BALL, :].astype(f32)
            mixed.append((wide + ball_attend(wide, w_in[0], w_out[0])).astype(bf16))
        if pair == 0:
            for copy in (*copies[3:], *extra):
                copy.wait()
        result = feed_forward(jnp.concatenate(mixed, 0), gate_up.at[0], down.at[0])
        out[pair : pair + 2 * BALL, :] = result.astype(bf16)


def picked_rows(slots, source, first_slot):
    want = lax.broadcasted_iota(jnp.int32, (BALL, 1), 0) + first_slot
    hot = jnp.where(want == slots, 1.0, 0.0).astype(bf16)
    return dot(hot, source)


def returned_rows(want, source, first_slot):
    hot = [
        jnp.where(want == first_slot + at, 1.0, 0.0).astype(bf16)
        for at in range(0, source.shape[0], LANES)
    ]
    return dot(jnp.concatenate(hot, 1), source)


def gather_rotated_kernel(spans, bases, *refs):
    count = len(spans)
    slots, sources, acc, out = refs[:4], refs[4 : 4 + count], refs[4 + count : -1], refs[-1]
    for i in range(2):
        here = slice(i * BALL, (i + 1) * BALL)
        first_slot = (2 * pl.program_id(0) + i) * BALL + bases[0]
        total = acc[0][here, :].astype(f32) if acc else None
        for (block, start, rows), source in zip(spans, sources):
            part = picked_rows(slots[block][:, start : start + rows], source[...], first_slot)
            total = part if total is None else total + part
        out[here, :] = total.astype(bf16)


def turn_kernel(spans, balls_before, bases, *refs):
    count = len(spans)
    slots, sources = refs[:4], refs[4 : 4 + count]
    acc, w_in, w_out = refs[4 + count : 7 + count]
    out = refs[-1]
    for i in range(acc.shape[0] // BALL):
        here = slice(i * BALL, (i + 1) * BALL)
        first_slot = (2 * pl.program_id(0) + i + balls_before) * BALL + bases[0]
        total = acc[here, :].astype(f32)
        for (block, start, rows), source in zip(spans, sources):
            total += picked_rows(slots[block][:, start : start + rows], source[...], first_slot)
        out[here, :] = ball_attend(total, w_in[0], w_out[0]).astype(bf16)


def last_turn_kernel(spans, near_spans, balls_before, bases, wanted, *refs):
    count, held = len(spans), len(near_spans) - 1
    sources = refs[7 + count : 7 + count + held]
    out, near = refs[-2:]
    turn_kernel(spans, balls_before, bases, *refs[: 7 + count], out)
    near_returned(near_spans, bases, wanted, (*sources, out), near)


def columns_kernel(slots, out):
    tall = jnp.broadcast_to(slots[0].astype(f32), (LANES, BALL)).T
    out[...] = tall.astype(jnp.int32) - lax.broadcasted_iota(jnp.int32, (BALL, LANES), 1)


def gather_returned_kernel(spans, bases, wanted, *refs):
    count = len(spans)
    sources, acc, out = refs[:count], refs[count:-1], refs[-1]
    want = wanted[...]
    total = acc[0][...].astype(f32) if acc else None
    for (block, start, rows), source in zip(spans, sources):
        part = returned_rows(want, source[...], bases[block] + start)
        total = part if total is None else total + part
    out[...] = total.astype(bf16)


def second_kernel(spans, bases, wanted, *refs):
    count = len(spans)
    sources = refs[:count]
    acc, first_a, first_b, first_c, gate_up, down, pool_weight = refs[count : count + 7]
    second, pooled, pooled_normed = refs[count + 7 : -2]
    tall = refs[-2:]
    step = pl.program_id(0)
    want = wanted[...]
    returned = acc[...].astype(f32)
    for (block, start, rows), source in zip(spans, sources):
        returned += returned_rows(want, source[...], bases[block] + start)
    inner = jnp.where(step == 0, first_a[...], first_b[...])
    first = jnp.where(step == pl.num_programs(0) - 1, first_c[...], inner)
    mixed = (first.astype(f32) + returned).astype(bf16)
    result = feed_forward(mixed, gate_up.at[0], down.at[0]).astype(bf16)
    second[...] = result
    size = acc.shape[0]
    here = pl.ds(pl.multiple_of(step * size, size), size)
    for half, ref in enumerate(tall):
        ref[here, :] = result[:, half * LANES : (half + 1) * LANES].astype(f32)

    @pl.when(step == pl.num_programs(0) - 1)
    def _():
        width = result.shape[1]
        count = pooled.shape[0]
        total = None
        for j in range(CHILDREN):
            child = jnp.concatenate(
                [ref[pl.ds(j, count, stride=CHILDREN), :].astype(bf16) for ref in tall], 1
            )
            part = dot(child, pool_weight[j * width : (j + 1) * width, :])
            total = part if total is None else total + part
        rounded = total.astype(bf16)
        pooled[...] = rounded
        pooled_normed[...] = normed(rounded.astype(f32))


def coarse_share(queries, sources, w_in, keys, values):
    width = queries.shape[1]
    at = 0
    for source in sources:
        rows = source.shape[0]
        pair = dot(source[...], w_in[:, width:])
        keys[at : at + rows, :] = pair[:, :width].astype(bf16)
        values[at : at + rows, :] = pair[:, width:].astype(bf16)
        at += rows
    part = width // 2
    shares = []
    for half in range(2):
        cols = slice(half * part, (half + 1) * part)
        share = None
        for mask, query in masked_heads(queries[:, cols], CHEADS // 2):
            scores = lax.dot_general(query, keys[:at, cols], LANES_BOTH, preferred_element_type=f32)
            most = jnp.max(scores, axis=-1, keepdims=True)
            scores = jnp.exp2(scores - most)
            total = jnp.sum(scores, axis=-1, keepdims=True)
            mixed = dot(scores.astype(bf16), values[:at, cols])
            if share is None:
                share = [mixed] + [jnp.broadcast_to(x, mixed.shape) for x in (most, total)]
            else:
                share = [jnp.where(mask, x, old) for x, old in zip((mixed, most, total), share)]
        shares.append(share)
    return [jnp.concatenate(pair, 1) for pair in zip(*shares)]


def coarse_early_kernel(blocks, *refs):
    sources = refs[:blocks]
    w_in, out_queries, mixture, most, total, keys, values = refs[blocks:]
    width = out_queries.shape[1]
    scale = LOG2E / math.sqrt(width // CHEADS)
    queries = (dot(sources[0][...], w_in[:, :width]) * scale).astype(bf16)
    out_queries[...] = queries
    mixture[...], most[...], total[...] = coarse_share(queries, sources, w_in, keys, values)


def coarse_kernel(blocks, *refs):
    sources, early = refs[:blocks], refs[blocks : blocks + 4]
    pooled, second, w_in, w_out, gate_up, down, unpool, out, keys, values = refs[blocks + 4 : -2]
    tall = refs[-2:]
    mixed_late, most_late, total_late = coarse_share(early[0][...], sources, w_in, keys, values)
    mixed, most, total = (ref[...] for ref in early[1:])
    top = jnp.maximum(most, most_late)
    keep, keep_late = jnp.exp2(most - top), jnp.exp2(most_late - top)
    mixture = (mixed * keep + mixed_late * keep_late) / (total * keep + total_late * keep_late)
    stream = (pooled[...].astype(f32) + dot(mixture.astype(bf16), w_out[...])).astype(bf16)
    coarse = feed_forward(stream, gate_up, down).astype(bf16)
    source = normed(coarse.astype(f32))
    count, fine = source.shape[0], second.shape[1]
    for j in range(CHILDREN):
        lifted = dot(source, unpool[:, j * fine : (j + 1) * fine])
        for half, ref in enumerate(tall):
            lanes = slice(half * LANES, (half + 1) * LANES)
            ref[pl.ds(j, count, stride=CHILDREN), :] = lifted[:, lanes]
    for half, ref in enumerate(tall):
        lanes = slice(half * LANES, (half + 1) * LANES)
        out[:, lanes] = (second[:, lanes].astype(f32) + ref[...]).astype(bf16)


def whole(shape):
    return pl.BlockSpec(shape, lambda *_: (0,) * len(shape))


def layer(shape, index):
    return pl.BlockSpec((1,) + shape[1:], lambda *_: (index, 0, 0))


def ball_rows(width, before=0):
    return pl.BlockSpec((BALL, width), lambda i: (i + before, 0))


def params(mib=20):
    return pltpu.CompilerParams(vmem_limit_bytes=mib << 20)


def cost(gflop, mbyte):
    return pl.CostEstimate(
        flops=int(gflop * 1e9), bytes_accessed=int(mbyte * 1e6), transcendentals=0
    )


def swap(value, axis):
    return lax.ppermute(value, axis, [(0, 1), (1, 0)])


def turn_y(value, distance):
    size = lax.axis_size("y")
    return lax.ppermute(value, "y", [(i, (i + distance) % size) for i in range(size)])


def after(value, *others):
    if not others:
        return value
    return lax.optimization_barrier((value, *others))[0]


def spans_of(blocks, counts, wanted):
    spans, arrays = [], []
    for block, chunk in wanted:
        start = sum(counts[:chunk]) * BALL
        spans.append((block, start, counts[chunk] * BALL))
        arrays.append(blocks[block][chunk])
    return tuple(spans), arrays


def local(
    points,
    rotated_slot,
    fine_attend_in,
    fine_attend_out,
    fine_gate_up,
    fine_down,
    pool_weight,
    coarse_attend_in,
    coarse_attend_out,
    coarse_gate_up,
    coarse_down,
    unpool_weight,
):
    rows, width = points.shape
    balls = rows // BALL
    cols = lax.axis_size("x") * lax.axis_size("w") * lax.axis_size("y")
    mine = lax.axis_index("z") * 2 + lax.axis_index("c")
    col = lax.axis_index(("x", "w", "y"))

    own_slot = rotated_slot.reshape(1, rows)
    far_slot = lax.ppermute(own_slot, ("z", "c"), [(0, 3), (1, 2), (2, 1), (3, 0)])
    group_slots = [own_slot, swap(own_slot, "c"), swap(own_slot, "z"), far_slot]
    bases = jnp.stack([((mine ^ flip) * cols + col) * rows for flip in (0, 1, 2, 3)]).astype(
        jnp.int32
    )
    smem = pl.BlockSpec(memory_space=pltpu.SMEM)

    weights = (fine_attend_in, fine_attend_out, fine_gate_up, fine_down)
    first_chunks, arrived, before = [], [], 0
    hbm = pl.BlockSpec(memory_space=pl.ANY)
    smem = pl.BlockSpec(memory_space=pltpu.SMEM)
    vmem = pl.BlockSpec(memory_space=pltpu.VMEM)

    def scratch(count):
        return (
            [pltpu.VMEM((count * BALL, width), bf16)]
            + [pltpu.VMEM((1,) + weight.shape[1:], bf16) for weight in weights]
            + [pltpu.SemaphoreType.DMA((5,))]
        )

    for count in FIRST_CHUNKS[:-1]:
        pending = []
        if first_chunks:
            pending = [first_chunks[-1]] + group_slots[1:]
            arrived.append(swap(after(first_chunks[-1], *arrived[-1:]), "z"))
        first_chunks.append(
            pl.pallas_call(
                functools.partial(first_kernel, before),
                name="first",
                in_specs=[hbm] * 5,
                out_specs=vmem,
                out_shape=jax.ShapeDtypeStruct((count * BALL, width), bf16),
                scratch_shapes=scratch(count),
                compiler_params=params(60),
                cost_estimate=cost(1.2 * count, 0.5),
            )(after(points, *pending), *weights)
        )
        before += count
    last = len(FIRST_CHUNKS) - 1
    arrived.append(swap(after(first_chunks[-1], *arrived[-1:]), "z"))
    count = FIRST_CHUNKS[-1]
    siblings = [swap(first_chunks[0], "c")]
    blocks = [first_chunks, siblings, arrived, []]
    spans, arrays = spans_of(blocks, FIRST_CHUNKS, [(0, 0), (0, 1), (1, 0), (2, 0)])
    spans += ((0, before * BALL, count * BALL),)
    chunk, near = pl.pallas_call(
        functools.partial(last_first_kernel, before, spans),
        name="first_near",
        in_specs=[smem] + [vmem] * 3 + [hbm] * (5 + len(arrays)),
        out_specs=[vmem, vmem],
        out_shape=[
            jax.ShapeDtypeStruct((count * BALL, width), bf16),
            jax.ShapeDtypeStruct((rows, width), bf16),
        ],
        scratch_shapes=[pltpu.VMEM(array.shape, bf16) for array in arrays]
        + [pltpu.SemaphoreType.DMA((len(arrays),))]
        + scratch(count),
        compiler_params=params(60),
        cost_estimate=cost(6, 2),
    )(bases, *group_slots[:3], points, *weights, *arrays)
    first_chunks.append(chunk)
    arrived.append(swap(after(chunk, arrived[-1]), "z"))
    siblings += [swap(after(first_chunks[1], chunk), "c"), swap(chunk, "c")]
    blocks[3].extend(swap(block, "c") for block in arrived[:-1])
    wanted = pl.pallas_call(
        columns_kernel,
        name="columns",
        grid=(balls,),
        in_specs=[pl.BlockSpec((1, 1, BALL), lambda i: (i, 0, 0))],
        out_specs=ball_rows(LANES),
        out_shape=jax.ShapeDtypeStruct((rows, LANES), jnp.int32),
        compiler_params=params(),
        cost_estimate=cost(0.5, 1),
    )(after(rotated_slot, first_chunks[-1]).reshape(balls, 1, BALL))

    two_balls = pl.BlockSpec((2 * BALL, width), lambda i: (i, 0))

    def gather_rotated(picked, acc):
        spans, arrays = spans_of(blocks, FIRST_CHUNKS, picked)
        return pl.pallas_call(
            functools.partial(gather_rotated_kernel, spans),
            name="gather_rotated",
            grid=(balls // 2,),
            in_specs=[smem]
            + [whole((1, rows))] * 4
            + [whole(array.shape) for array in arrays]
            + [two_balls] * len(acc),
            out_specs=two_balls,
            out_shape=jax.ShapeDtypeStruct((rows, width), bf16),
            compiler_params=params(),
            cost_estimate=cost(7, 4),
        )(bases, *group_slots, *arrays, *acc)

    rest = [(3, 0), (1, 1), (1, 2), (2, 1), (3, 1)]
    acc = gather_rotated(rest, [near])
    blocks[3].append(swap(after(blocks[2][last], acc), "c"))
    spans, arrays = spans_of(blocks, FIRST_CHUNKS, [(2, last), (3, last)])
    turned_chunks, arrived, before = [], [], 0
    for place, count in enumerate(TURN_CHUNKS):
        final = place == last
        kernel = functools.partial(turn_kernel, spans, before)
        extra, extra_specs = turned_chunks[-1:], [hbm] * len(turned_chunks[-1:])
        out_specs = [pl.BlockSpec((2 * BALL, width), lambda i: (i, 0))]
        out_shape = [jax.ShapeDtypeStruct((count * BALL, width), bf16)]
        columns, column_specs = [], []
        if final:
            siblings = [swap(turned_chunks[0], "c")]
            back = [turned_chunks, siblings, arrived, []]
            near_spans, extra = spans_of(back, TURN_CHUNKS, [(0, 0), (0, 1), (1, 0), (2, 0)])
            near_spans += ((0, before * BALL, count * BALL),)
            kernel = functools.partial(last_turn_kernel, spans, near_spans, before)
            extra_specs = [whole(array.shape) for array in extra]
            columns, column_specs = [wanted], [whole(wanted.shape)]
            out_specs.append(whole((rows, width)))
            out_shape.append(jax.ShapeDtypeStruct((rows, width), bf16))
        result = pl.pallas_call(
            kernel,
            name="turn_near" if final else "turn",
            grid=(count // 2,),
            in_specs=[smem]
            + column_specs
            + [whole((1, rows))] * 4
            + [whole(array.shape) for array in arrays]
            + [
                pl.BlockSpec((2 * BALL, width), lambda i, b=before // 2: (i + b, 0)),
                layer(fine_attend_in.shape, 1),
                layer(fine_attend_out.shape, 1),
            ]
            + extra_specs,
            out_specs=out_specs,
            out_shape=out_shape,
            compiler_params=params(),
            cost_estimate=cost(6 if final else 1.2 * count, 0.5),
        )(
            bases,
            *columns,
            *group_slots,
            *arrays,
            acc,
            fine_attend_in,
            fine_attend_out,
            *extra,
        )
        turned_chunks.append(result[0])
        arrived.append(swap(after(result[0], *arrived[-1:]), "z"))
        before += count
    near = result[1]
    siblings += [swap(after(turned_chunks[1], result[0]), "c"), swap(result[0], "c")]
    back[3].extend(swap(block, "c") for block in arrived[:-1])
    last = len(TURN_CHUNKS) - 1

    def gather_returned(picked, acc):
        spans, arrays = spans_of(back, TURN_CHUNKS, picked)
        return pl.pallas_call(
            functools.partial(gather_returned_kernel, spans),
            name="gather_returned",
            grid=(balls // 2,),
            in_specs=[smem, pl.BlockSpec((2 * BALL, LANES), lambda i: (i, 0))]
            + [whole(array.shape) for array in arrays]
            + [two_balls] * len(acc),
            out_specs=two_balls,
            out_shape=jax.ShapeDtypeStruct((rows, width), bf16),
            compiler_params=params(),
            cost_estimate=cost(7, 4),
        )(bases, wanted, *arrays, *acc)

    acc = gather_returned(rest, [near])
    back[3].append(swap(after(back[2][last], acc), "c"))
    spans, arrays = spans_of(back, TURN_CHUNKS, [(2, last), (3, last)])
    pooled_rows, coarse_width = rows // CHILDREN, pool_weight.shape[1]
    second, pooled, pooled_normed = pl.pallas_call(
        functools.partial(second_kernel, spans),
        name="second",
        grid=(balls // 2,),
        in_specs=[smem, pl.BlockSpec((2 * BALL, LANES), lambda i: (i, 0))]
        + [whole(array.shape) for array in arrays]
        + [
            two_balls,
            pl.BlockSpec((2 * BALL, width), lambda i: (0, 0)),
            pl.BlockSpec((2 * BALL, width), lambda i: (jnp.clip(i - 1, 0, 1), 0)),
            pl.BlockSpec((2 * BALL, width), lambda i: (0, 0)),
            layer(fine_gate_up.shape, 1),
            layer(fine_down.shape, 1),
            whole(pool_weight.shape),
        ],
        out_specs=[
            two_balls,
            whole((pooled_rows, coarse_width)),
            whole((pooled_rows, coarse_width)),
        ],
        out_shape=[
            jax.ShapeDtypeStruct((rows, width), bf16),
            jax.ShapeDtypeStruct((pooled_rows, coarse_width), bf16),
            jax.ShapeDtypeStruct((pooled_rows, coarse_width), bf16),
        ],
        scratch_shapes=[pltpu.VMEM((rows, LANES), f32)] * 2,
        compiler_params=params(),
        cost_estimate=cost(8, 4),
    )(bases, wanted, *arrays, acc, *first_chunks, fine_gate_up, fine_down, pool_weight)

    other = swap(pooled_normed, "w")
    opposite = turn_y(pooled_normed, 2)
    up, down_y = turn_y(pooled_normed, 1), turn_y(pooled_normed, -1)
    late = [up, down_y, turn_y(other, 1), turn_y(other, -1), swap(opposite, "w")]
    soon = [pooled_normed, other, opposite]
    square = (pooled_rows, coarse_width)
    held = [pltpu.VMEM((pooled_rows * len(late), coarse_width), bf16)] * 2
    early = pl.pallas_call(
        functools.partial(coarse_early_kernel, len(soon)),
        name="coarse_early",
        grid=(1,),
        in_specs=[whole(square)] * len(soon) + [whole(coarse_attend_in.shape)],
        out_specs=[whole(square)] * 4,
        out_shape=[jax.ShapeDtypeStruct(square, bf16)] + [jax.ShapeDtypeStruct(square, f32)] * 3,
        scratch_shapes=held,
        compiler_params=params(),
        cost_estimate=cost(5, 4),
    )(*soon, coarse_attend_in)
    operands = [
        *late,
        *early,
        pooled,
        second,
        coarse_attend_in,
        coarse_attend_out,
        coarse_gate_up,
        coarse_down,
        unpool_weight,
    ]
    return pl.pallas_call(
        functools.partial(coarse_kernel, len(late)),
        name="coarse",
        grid=(1,),
        in_specs=[whole(array.shape) for array in operands],
        out_specs=whole((rows, width)),
        out_shape=jax.ShapeDtypeStruct((rows, width), bf16),
        scratch_shapes=held + [pltpu.VMEM((rows, LANES), f32)] * 2,
        compiler_params=params(40),
        cost_estimate=cost(8, 16),
    )(*operands)


def solution(mesh):
    torus = Mesh(mesh.devices.reshape(2, 2, 4, 2, 4), AXES)
    split = P(AXES, None)
    return jax.shard_map(
        local,
        mesh=torus,
        in_specs=(split, P(AXES)) + (P(),) * 10,
        out_specs=split,
        check_vma=False,
    )
```

```python
import functools
import math

import jax
import jax.numpy as jnp
from jax import lax
from jax.experimental import pallas as pl
from jax.experimental.pallas import tpu as pltpu
from jax.sharding import Mesh
from jax.sharding import PartitionSpec as P

HEADS = 8
CHEADS = 8
BALL = 256
CHILDREN = 8
LANES = 128
EPSILON = 1e-06
LOG2E = 1.4426950408889634
AXES = ("z", "c", "x", "w", "y")
FIRST_CHUNKS = (2, 4, 2)
TURN_CHUNKS = (2, 4, 2)

f32 = jnp.float32
bf16 = jnp.bfloat16
LANES_BOTH = (((1,), (1,)), ((), ()))


def dot(a, b):
    return jnp.dot(a, b, preferred_element_type=f32)


def normed(wide):
    return (wide * lax.rsqrt(jnp.mean(wide * wide, axis=-1, keepdims=True) + EPSILON)).astype(bf16)


def gated(gate, up):
    half = 0.5 * gate
    return (half * up * (1.0 + jnp.tanh(half))).astype(bf16)


def masked_heads(value, heads):
    width = value.shape[1]
    lane = lax.broadcasted_iota(jnp.int32, (1, width), 1) // (width // heads)
    return [(lane == h, jnp.where(lane == h, value, jnp.zeros_like(value))) for h in range(heads)]


def ball_attend(wide, w_in, w_out):
    width = wide.shape[1]
    packed = dot(normed(wide), w_in)
    scale = LOG2E / math.sqrt(width // HEADS)
    queries = (packed[:, :width] * scale).astype(bf16)
    keys = packed[:, width : 2 * width].astype(bf16)
    values = packed[:, 2 * width :].astype(bf16)
    weights, shares, inverse = [], [], None
    for (mask, query), (_, value) in zip(
        masked_heads(queries, HEADS), masked_heads(values, HEADS)
    ):
        scores = lax.dot_general(query, keys, LANES_BOTH, preferred_element_type=f32)
        scores = jnp.exp2(scores - jnp.max(scores, axis=-1, keepdims=True))
        total = 1.0 / jnp.sum(scores, axis=-1, keepdims=True)
        if inverse is None:
            inverse = jnp.broadcast_to(total, wide.shape)
        else:
            inverse = jnp.where(mask, total, inverse)
        weights.append(scores.astype(bf16))
        shares.append(value)
    mixture = dot(jnp.concatenate(weights, 1), jnp.concatenate(shares, 0)) * inverse
    return dot(mixture.astype(bf16), w_out)


def feed_forward(stream, gate_up, down):
    wide = stream.astype(f32)
    half = down.shape[0]
    source = normed(wide)
    hidden = gated(dot(source, gate_up[:, :half]), dot(source, gate_up[:, half:]))
    return wide + dot(hidden, down[...])


def near_rotated(spans, bases, slots, sources, out):
    @pl.loop(0, out.shape[0] // (2 * BALL))
    def _(step):
        for i in range(2):
            ball = 2 * step + i
            total = None
            for (block, start, rows), source in zip(spans, sources):
                at = slots[block][:, start : start + rows]
                part = picked_rows(at, source[...], ball * BALL + bases[0])
                total = part if total is None else total + part
            here = pl.ds(pl.multiple_of(ball * BALL, BALL), BALL)
            out[here, :] = total.astype(bf16)


def near_returned(spans, bases, wanted, sources, out):
    @pl.loop(0, out.shape[0] // (2 * BALL))
    def _(step):
        here = pl.ds(pl.multiple_of(step * 2 * BALL, 2 * BALL), 2 * BALL)
        want, total = wanted[here, :], None
        for (block, start, rows), source in zip(spans, sources):
            part = returned_rows(want, source[...], bases[block] + start)
            total = part if total is None else total + part
        out[here, :] = total.astype(bf16)


def last_first_kernel(before, spans, bases, slot_own, slot_core, slot_z, *refs):
    count = len(spans) - 1
    own, sources = refs[:5], refs[5 : 5 + count]
    out, near, held = refs[5 + count], refs[6 + count], refs[7 + count : 7 + 2 * count]
    sems = refs[7 + 2 * count]
    copies = [
        pltpu.make_async_copy(source, ref, sems.at[i])
        for i, (source, ref) in enumerate(zip(sources, held))
    ]
    first_kernel(before, *own, out, *refs[8 + 2 * count :], extra=copies)
    near_rotated(spans, bases, (slot_own, slot_core, slot_z), (*held, out), near)


def first_kernel(before, points, w_in, w_out, gate_up, down, *refs, extra=()):
    out, held, sems = refs[-7], refs[-6:-1], refs[-1]
    sources = (
        points.at[pl.ds(before * BALL, out.shape[0]), :],
        *(ref.at[pl.ds(0, 1)] for ref in (w_in, w_out, gate_up, down)),
    )
    copies = [
        pltpu.make_async_copy(source, ref, sems.at[i])
        for i, (source, ref) in enumerate(zip(sources, held))
    ]
    for copy in copies:
        copy.start()
    for copy in extra:
        copy.start()
    for copy in copies[:3]:
        copy.wait()
    rows, w_in, w_out, gate_up, down = held
    for pair in range(0, out.shape[0], 2 * BALL):
        mixed = []
        for at in range(pair, pair + 2 * BALL, BALL):
            wide = rows[at : at + BALL, :].astype(f32)
            mixed.append((wide + ball_attend(wide, w_in[0], w_out[0])).astype(bf16))
        if pair == 0:
            for copy in (*copies[3:], *extra):
                copy.wait()
        result = feed_forward(jnp.concatenate(mixed, 0), gate_up.at[0], down.at[0])
        out[pair : pair + 2 * BALL, :] = result.astype(bf16)


def picked_rows(slots, source, first_slot):
    want = lax.broadcasted_iota(jnp.int32, (BALL, 1), 0) + first_slot
    hot = jnp.where(want == slots, 1.0, 0.0).astype(bf16)
    return dot(hot, source)


def returned_rows(want, source, first_slot):
    hot = [
        jnp.where(want == first_slot + at, 1.0, 0.0).astype(bf16)
        for at in range(0, source.shape[0], LANES)
    ]
    return dot(jnp.concatenate(hot, 1), source)


def gather_rotated_kernel(spans, bases, *refs):
    count = len(spans)
    slots, sources, acc, out = refs[:4], refs[4 : 4 + count], refs[4 + count : -1], refs[-1]
    for i in range(2):
        here = slice(i * BALL, (i + 1) * BALL)
        first_slot = (2 * pl.program_id(0) + i) * BALL + bases[0]
        total = acc[0][here, :].astype(f32) if acc else None
        for (block, start, rows), source in zip(spans, sources):
            part = picked_rows(slots[block][:, start : start + rows], source[...], first_slot)
            total = part if total is None else total + part
        out[here, :] = total.astype(bf16)


def turn_kernel(spans, balls_before, bases, *refs):
    count = len(spans)
    slots, sources = refs[:4], refs[4 : 4 + count]
    acc, w_in, w_out = refs[4 + count : 7 + count]
    out = refs[-1]
    for i in range(acc.shape[0] // BALL):
        here = slice(i * BALL, (i + 1) * BALL)
        first_slot = (2 * pl.program_id(0) + i + balls_before) * BALL + bases[0]
        total = acc[here, :].astype(f32)
        for (block, start, rows), source in zip(spans, sources):
            total += picked_rows(slots[block][:, start : start + rows], source[...], first_slot)
        out[here, :] = ball_attend(total, w_in[0], w_out[0]).astype(bf16)


def last_turn_kernel(spans, near_spans, balls_before, bases, wanted, *refs):
    count, held = len(spans), len(near_spans) - 1
    sources = refs[7 + count : 7 + count + held]
    out, near = refs[-2:]
    turn_kernel(spans, balls_before, bases, *refs[: 7 + count], out)
    near_returned(near_spans, bases, wanted, (*sources, out), near)


def columns_kernel(slots, out):
    tall = jnp.broadcast_to(slots[0].astype(f32), (LANES, BALL)).T
    out[...] = tall.astype(jnp.int32) - lax.broadcasted_iota(jnp.int32, (BALL, LANES), 1)


def gather_returned_kernel(spans, bases, wanted, *refs):
    count = len(spans)
    sources, acc, out = refs[:count], refs[count:-1], refs[-1]
    want = wanted[...]
    total = acc[0][...].astype(f32) if acc else None
    for (block, start, rows), source in zip(spans, sources):
        part = returned_rows(want, source[...], bases[block] + start)
        total = part if total is None else total + part
    out[...] = total.astype(bf16)


def second_kernel(spans, bases, wanted, *refs):
    count = len(spans)
    sources = refs[:count]
    acc, first_a, first_b, first_c, gate_up, down, pool_weight = refs[count : count + 7]
    second, pooled, pooled_normed = refs[count + 7 : -2]
    tall = refs[-2:]
    step = pl.program_id(0)
    want = wanted[...]
    returned = acc[...].astype(f32)
    for (block, start, rows), source in zip(spans, sources):
        returned += returned_rows(want, source[...], bases[block] + start)
    inner = jnp.where(step == 0, first_a[...], first_b[...])
    first = jnp.where(step == pl.num_programs(0) - 1, first_c[...], inner)
    mixed = (first.astype(f32) + returned).astype(bf16)
    result = feed_forward(mixed, gate_up.at[0], down.at[0]).astype(bf16)
    second[...] = result
    size = acc.shape[0]
    here = pl.ds(pl.multiple_of(step * size, size), size)
    for half, ref in enumerate(tall):
        ref[here, :] = result[:, half * LANES : (half + 1) * LANES].astype(f32)

    @pl.when(step == pl.num_programs(0) - 1)
    def _():
        width = result.shape[1]
        count = pooled.shape[0]
        total = None
        for j in range(CHILDREN):
            child = jnp.concatenate(
                [ref[pl.ds(j, count, stride=CHILDREN), :].astype(bf16) for ref in tall], 1
            )
            part = dot(child, pool_weight[j * width : (j + 1) * width, :])
            total = part if total is None else total + part
        rounded = total.astype(bf16)
        pooled[...] = rounded
        pooled_normed[...] = normed(rounded.astype(f32))


def coarse_share(queries, sources, w_in, keys, values):
    width = queries.shape[1]
    at = 0
    for source in sources:
        rows = source.shape[0]
        pair = dot(source[...], w_in[:, width:])
        keys[at : at + rows, :] = pair[:, :width].astype(bf16)
        values[at : at + rows, :] = pair[:, width:].astype(bf16)
        at += rows
    part = width // 2
    shares = []
    for half in range(2):
        cols = slice(half * part, (half + 1) * part)
        share = None
        for mask, query in masked_heads(queries[:, cols], CHEADS // 2):
            scores = lax.dot_general(query, keys[:at, cols], LANES_BOTH, preferred_element_type=f32)
            most = jnp.max(scores, axis=-1, keepdims=True)
            scores = jnp.exp2(scores - most)
            total = jnp.sum(scores, axis=-1, keepdims=True)
            mixed = dot(scores.astype(bf16), values[:at, cols])
            if share is None:
                share = [mixed] + [jnp.broadcast_to(x, mixed.shape) for x in (most, total)]
            else:
                share = [jnp.where(mask, x, old) for x, old in zip((mixed, most, total), share)]
        shares.append(share)
    return [jnp.concatenate(pair, 1) for pair in zip(*shares)]


def coarse_early_kernel(blocks, *refs):
    sources = refs[:blocks]
    w_in, out_queries, mixture, most, total, keys, values = refs[blocks:]
    width = out_queries.shape[1]
    scale = LOG2E / math.sqrt(width // CHEADS)
    queries = (dot(sources[0][...], w_in[:, :width]) * scale).astype(bf16)
    out_queries[...] = queries
    mixture[...], most[...], total[...] = coarse_share(queries, sources, w_in, keys, values)


def coarse_kernel(blocks, *refs):
    sources, early = refs[:blocks], refs[blocks : blocks + 4]
    pooled, second, w_in, w_out, gate_up, down, unpool, out, keys, values = refs[blocks + 4 : -2]
    tall = refs[-2:]
    mixed_late, most_late, total_late = coarse_share(early[0][...], sources, w_in, keys, values)
    mixed, most, total = (ref[...] for ref in early[1:])
    top = jnp.maximum(most, most_late)
    keep, keep_late = jnp.exp2(most - top), jnp.exp2(most_late - top)
    mixture = (mixed * keep + mixed_late * keep_late) / (total * keep + total_late * keep_late)
    stream = (pooled[...].astype(f32) + dot(mixture.astype(bf16), w_out[...])).astype(bf16)
    coarse = feed_forward(stream, gate_up, down).astype(bf16)
    source = normed(coarse.astype(f32))
    count, fine = source.shape[0], second.shape[1]
    for j in range(CHILDREN):
        lifted = dot(source, unpool[:, j * fine : (j + 1) * fine])
        for half, ref in enumerate(tall):
            lanes = slice(half * LANES, (half + 1) * LANES)
            ref[pl.ds(j, count, stride=CHILDREN), :] = lifted[:, lanes]
    for half, ref in enumerate(tall):
        lanes = slice(half * LANES, (half + 1) * LANES)
        out[:, lanes] = (second[:, lanes].astype(f32) + ref[...]).astype(bf16)


def whole(shape):
    return pl.BlockSpec(shape, lambda *_: (0,) * len(shape))


def layer(shape, index):
    return pl.BlockSpec((1,) + shape[1:], lambda *_: (index, 0, 0))


def ball_rows(width, before=0):
    return pl.BlockSpec((BALL, width), lambda i: (i + before, 0))


def params(mib=20):
    return pltpu.CompilerParams(vmem_limit_bytes=mib << 20)


def cost(gflop, mbyte):
    return pl.CostEstimate(
        flops=int(gflop * 1e9), bytes_accessed=int(mbyte * 1e6), transcendentals=0
    )


def swap(value, axis):
    return lax.ppermute(value, axis, [(0, 1), (1, 0)])


def turn_y(value, distance):
    size = lax.axis_size("y")
    return lax.ppermute(value, "y", [(i, (i + distance) % size) for i in range(size)])


def after(value, *others):
    if not others:
        return value
    return lax.optimization_barrier((value, *others))[0]


def spans_of(blocks, counts, wanted):
    spans, arrays = [], []
    for block, chunk in wanted:
        start = sum(counts[:chunk]) * BALL
        spans.append((block, start, counts[chunk] * BALL))
        arrays.append(blocks[block][chunk])
    return tuple(spans), arrays


def local(
    points,
    rotated_slot,
    fine_attend_in,
    fine_attend_out,
    fine_gate_up,
    fine_down,
    pool_weight,
    coarse_attend_in,
    coarse_attend_out,
    coarse_gate_up,
    coarse_down,
    unpool_weight,
):
    rows, width = points.shape
    balls = rows // BALL
    cols = lax.axis_size("x") * lax.axis_size("w") * lax.axis_size("y")
    mine = lax.axis_index("z") * 2 + lax.axis_index("c")
    col = lax.axis_index(("x", "w", "y"))

    own_slot = rotated_slot.reshape(1, rows)
    far_slot = lax.ppermute(own_slot, ("z", "c"), [(0, 3), (1, 2), (2, 1), (3, 0)])
    group_slots = [own_slot, swap(own_slot, "c"), swap(own_slot, "z"), far_slot]
    bases = jnp.stack([((mine ^ flip) * cols + col) * rows for flip in (0, 1, 2, 3)]).astype(
        jnp.int32
    )
    smem = pl.BlockSpec(memory_space=pltpu.SMEM)

    weights = (fine_attend_in, fine_attend_out, fine_gate_up, fine_down)
    first_chunks, arrived, before = [], [], 0
    hbm = pl.BlockSpec(memory_space=pl.ANY)
    smem = pl.BlockSpec(memory_space=pltpu.SMEM)
    vmem = pl.BlockSpec(memory_space=pltpu.VMEM)

    def scratch(count):
        return (
            [pltpu.VMEM((count * BALL, width), bf16)]
            + [pltpu.VMEM((1,) + weight.shape[1:], bf16) for weight in weights]
            + [pltpu.SemaphoreType.DMA((5,))]
        )

    for count in FIRST_CHUNKS[:-1]:
        pending = []
        if first_chunks:
            pending = [first_chunks[-1]] + group_slots[1:]
            arrived.append(swap(after(first_chunks[-1], *arrived[-1:]), "z"))
        first_chunks.append(
            pl.pallas_call(
                functools.partial(first_kernel, before),
                name="first",
                in_specs=[hbm] * 5,
                out_specs=vmem,
                out_shape=jax.ShapeDtypeStruct((count * BALL, width), bf16),
                scratch_shapes=scratch(count),
                compiler_params=params(60),
                cost_estimate=cost(1.2 * count, 0.5),
            )(after(points, *pending), *weights)
        )
        before += count
    last = len(FIRST_CHUNKS) - 1
    arrived.append(swap(after(first_chunks[-1], *arrived[-1:]), "z"))
    count = FIRST_CHUNKS[-1]
    siblings = [swap(first_chunks[0], "c")]
    blocks = [first_chunks, siblings, arrived, []]
    spans, arrays = spans_of(blocks, FIRST_CHUNKS, [(0, 0), (0, 1), (1, 0), (2, 0)])
    spans += ((0, before * BALL, count * BALL),)
    chunk, near = pl.pallas_call(
        functools.partial(last_first_kernel, before, spans),
        name="first_near",
        in_specs=[smem] + [vmem] * 3 + [hbm] * (5 + len(arrays)),
        out_specs=[vmem, vmem],
        out_shape=[
            jax.ShapeDtypeStruct((count * BALL, width), bf16),
            jax.ShapeDtypeStruct((rows, width), bf16),
        ],
        scratch_shapes=[pltpu.VMEM(array.shape, bf16) for array in arrays]
        + [pltpu.SemaphoreType.DMA((len(arrays),))]
        + scratch(count),
        compiler_params=params(60),
        cost_estimate=cost(6, 2),
    )(bases, *group_slots[:3], points, *weights, *arrays)
    first_chunks.append(chunk)
    arrived.append(swap(after(chunk, arrived[-1]), "z"))
    siblings += [swap(after(first_chunks[1], chunk), "c"), swap(chunk, "c")]
    blocks[3].extend(swap(block, "c") for block in arrived[:-1])
    wanted = pl.pallas_call(
        columns_kernel,
        name="columns",
        grid=(balls,),
        in_specs=[pl.BlockSpec((1, 1, BALL), lambda i: (i, 0, 0))],
        out_specs=ball_rows(LANES),
        out_shape=jax.ShapeDtypeStruct((rows, LANES), jnp.int32),
        compiler_params=params(),
        cost_estimate=cost(0.5, 1),
    )(after(rotated_slot, first_chunks[-1]).reshape(balls, 1, BALL))

    two_balls = pl.BlockSpec((2 * BALL, width), lambda i: (i, 0))

    def gather_rotated(picked, acc):
        spans, arrays = spans_of(blocks, FIRST_CHUNKS, picked)
        return pl.pallas_call(
            functools.partial(gather_rotated_kernel, spans),
            name="gather_rotated",
            grid=(balls // 2,),
            in_specs=[smem]
            + [whole((1, rows))] * 4
            + [whole(array.shape) for array in arrays]
            + [two_balls] * len(acc),
            out_specs=two_balls,
            out_shape=jax.ShapeDtypeStruct((rows, width), bf16),
            compiler_params=params(),
            cost_estimate=cost(7, 4),
        )(bases, *group_slots, *arrays, *acc)

    rest = [(3, 0), (1, 1), (1, 2), (2, 1), (3, 1)]
    acc = gather_rotated(rest, [near])
    blocks[3].append(swap(after(blocks[2][last], acc), "c"))
    spans, arrays = spans_of(blocks, FIRST_CHUNKS, [(2, last), (3, last)])
    turned_chunks, arrived, before = [], [], 0
    for place, count in enumerate(TURN_CHUNKS):
        final = place == last
        kernel = functools.partial(turn_kernel, spans, before)
        extra, extra_specs = turned_chunks[-1:], [hbm] * len(turned_chunks[-1:])
        out_specs = [pl.BlockSpec((2 * BALL, width), lambda i: (i, 0))]
        out_shape = [jax.ShapeDtypeStruct((count * BALL, width), bf16)]
        columns, column_specs = [], []
        if final:
            siblings = [swap(turned_chunks[0], "c")]
            back = [turned_chunks, siblings, arrived, []]
            near_spans, extra = spans_of(back, TURN_CHUNKS, [(0, 0), (0, 1), (1, 0), (2, 0)])
            near_spans += ((0, before * BALL, count * BALL),)
            kernel = functools.partial(last_turn_kernel, spans, near_spans, before)
            extra_specs = [whole(array.shape) for array in extra]
            columns, column_specs = [wanted], [whole(wanted.shape)]
            out_specs.append(whole((rows, width)))
            out_shape.append(jax.ShapeDtypeStruct((rows, width), bf16))
        result = pl.pallas_call(
            kernel,
            name="turn_near" if final else "turn",
            grid=(count // 2,),
            in_specs=[smem]
            + column_specs
            + [whole((1, rows))] * 4
            + [whole(array.shape) for array in arrays]
            + [
                pl.BlockSpec((2 * BALL, width), lambda i, b=before // 2: (i + b, 0)),
                layer(fine_attend_in.shape, 1),
                layer(fine_attend_out.shape, 1),
            ]
            + extra_specs,
            out_specs=out_specs,
            out_shape=out_shape,
            compiler_params=params(),
            cost_estimate=cost(6 if final else 1.2 * count, 0.5),
        )(
            bases,
            *columns,
            *group_slots,
            *arrays,
            acc,
            fine_attend_in,
            fine_attend_out,
            *extra,
        )
        turned_chunks.append(result[0])
        arrived.append(swap(after(result[0], *arrived[-1:]), "z"))
        before += count
    near = result[1]
    siblings += [swap(after(turned_chunks[1], result[0]), "c"), swap(result[0], "c")]
    back[3].extend(swap(block, "c") for block in arrived[:-1])
    last = len(TURN_CHUNKS) - 1

    def gather_returned(picked, acc):
        spans, arrays = spans_of(back, TURN_CHUNKS, picked)
        return pl.pallas_call(
            functools.partial(gather_returned_kernel, spans),
            name="gather_returned",
            grid=(balls // 2,),
            in_specs=[smem, pl.BlockSpec((2 * BALL, LANES), lambda i: (i, 0))]
            + [whole(array.shape) for array in arrays]
            + [two_balls] * len(acc),
            out_specs=two_balls,
            out_shape=jax.ShapeDtypeStruct((rows, width), bf16),
            compiler_params=params(),
            cost_estimate=cost(7, 4),
        )(bases, wanted, *arrays, *acc)

    acc = gather_returned(rest, [near])
    back[3].append(swap(after(back[2][last], acc), "c"))
    spans, arrays = spans_of(back, TURN_CHUNKS, [(2, last), (3, last)])
    pooled_rows, coarse_width = rows // CHILDREN, pool_weight.shape[1]
    second, pooled, pooled_normed = pl.pallas_call(
        functools.partial(second_kernel, spans),
        name="second",
        grid=(balls // 2,),
        in_specs=[smem, pl.BlockSpec((2 * BALL, LANES), lambda i: (i, 0))]
        + [whole(array.shape) for array in arrays]
        + [
            two_balls,
            pl.BlockSpec((2 * BALL, width), lambda i: (0, 0)),
            pl.BlockSpec((2 * BALL, width), lambda i: (jnp.clip(i - 1, 0, 1), 0)),
            pl.BlockSpec((2 * BALL, width), lambda i: (0, 0)),
            layer(fine_gate_up.shape, 1),
            layer(fine_down.shape, 1),
            whole(pool_weight.shape),
        ],
        out_specs=[
            two_balls,
            whole((pooled_rows, coarse_width)),
            whole((pooled_rows, coarse_width)),
        ],
        out_shape=[
            jax.ShapeDtypeStruct((rows, width), bf16),
            jax.ShapeDtypeStruct((pooled_rows, coarse_width), bf16),
            jax.ShapeDtypeStruct((pooled_rows, coarse_width), bf16),
        ],
        scratch_shapes=[pltpu.VMEM((rows, LANES), f32)] * 2,
        compiler_params=params(),
        cost_estimate=cost(8, 4),
    )(bases, wanted, *arrays, acc, *first_chunks, fine_gate_up, fine_down, pool_weight)

    other = swap(pooled_normed, "w")
    opposite = turn_y(pooled_normed, 2)
    up, down_y = turn_y(pooled_normed, 1), turn_y(pooled_normed, -1)
    late = [turn_y(other, 1), turn_y(other, -1), swap(opposite, "w")]
    soon = [pooled_normed, other, opposite, up, down_y]
    square = (pooled_rows, coarse_width)
    held = [pltpu.VMEM((pooled_rows * len(soon), coarse_width), bf16)] * 2
    early = pl.pallas_call(
        functools.partial(coarse_early_kernel, len(soon)),
        name="coarse_early",
        grid=(1,),
        in_specs=[whole(square)] * len(soon) + [whole(coarse_attend_in.shape)],
        out_specs=[whole(square)] * 4,
        out_shape=[jax.ShapeDtypeStruct(square, bf16)] + [jax.ShapeDtypeStruct(square, f32)] * 3,
        scratch_shapes=held,
        compiler_params=params(),
        cost_estimate=cost(5, 4),
    )(*soon, coarse_attend_in)
    operands = [
        *late,
        *early,
        pooled,
        second,
        coarse_attend_in,
        coarse_attend_out,
        coarse_gate_up,
        coarse_down,
        unpool_weight,
    ]
    return pl.pallas_call(
        functools.partial(coarse_kernel, len(late)),
        name="coarse",
        grid=(1,),
        in_specs=[whole(array.shape) for array in operands],
        out_specs=whole((rows, width)),
        out_shape=jax.ShapeDtypeStruct((rows, width), bf16),
        scratch_shapes=held + [pltpu.VMEM((rows, LANES), f32)] * 2,
        compiler_params=params(40),
        cost_estimate=cost(8, 16),
    )(*operands)


def solution(mesh):
    torus = Mesh(mesh.devices.reshape(2, 2, 4, 2, 4), AXES)
    split = P(AXES, None)
    return jax.shard_map(
        local,
        mesh=torus,
        in_specs=(split, P(AXES)) + (P(),) * 10,
        out_specs=split,
        check_vma=False,
    )
```

```python
import functools
import math

import jax
import jax.numpy as jnp
from jax import lax
from jax.experimental import pallas as pl
from jax.experimental.pallas import tpu as pltpu
from jax.sharding import Mesh
from jax.sharding import PartitionSpec as P

HEADS = 8
CHEADS = 8
BALL = 256
CHILDREN = 8
LANES = 128
EPSILON = 1e-06
LOG2E = 1.4426950408889634
AXES = ("z", "c", "x", "w", "y")
FIRST_CHUNKS = (2, 4, 2)
TURN_CHUNKS = (2, 4, 2)

f32 = jnp.float32
bf16 = jnp.bfloat16
LANES_BOTH = (((1,), (1,)), ((), ()))


def dot(a, b):
    return jnp.dot(a, b, preferred_element_type=f32)


def normed(wide):
    return (wide * lax.rsqrt(jnp.mean(wide * wide, axis=-1, keepdims=True) + EPSILON)).astype(bf16)


def gated(gate, up):
    half = 0.5 * gate
    return (half * up * (1.0 + jnp.tanh(half))).astype(bf16)


def masked_heads(value, heads):
    width = value.shape[1]
    lane = lax.broadcasted_iota(jnp.int32, (1, width), 1) // (width // heads)
    return [(lane == h, jnp.where(lane == h, value, jnp.zeros_like(value))) for h in range(heads)]


def ball_attend(wide, w_in, w_out):
    width = wide.shape[1]
    packed = dot(normed(wide), w_in)
    scale = LOG2E / math.sqrt(width // HEADS)
    queries = (packed[:, :width] * scale).astype(bf16)
    keys = packed[:, width : 2 * width].astype(bf16)
    values = packed[:, 2 * width :].astype(bf16)
    weights, shares, inverse = [], [], None
    for (mask, query), (_, value) in zip(
        masked_heads(queries, HEADS), masked_heads(values, HEADS)
    ):
        scores = lax.dot_general(query, keys, LANES_BOTH, preferred_element_type=f32)
        scores = jnp.exp2(scores - jnp.max(scores, axis=-1, keepdims=True))
        total = 1.0 / jnp.sum(scores, axis=-1, keepdims=True)
        if inverse is None:
            inverse = jnp.broadcast_to(total, wide.shape)
        else:
            inverse = jnp.where(mask, total, inverse)
        weights.append(scores.astype(bf16))
        shares.append(value)
    mixture = dot(jnp.concatenate(weights, 1), jnp.concatenate(shares, 0)) * inverse
    return dot(mixture.astype(bf16), w_out)


def feed_forward(stream, gate_up, down):
    wide = stream.astype(f32)
    half = down.shape[0]
    source = normed(wide)
    hidden = gated(dot(source, gate_up[:, :half]), dot(source, gate_up[:, half:]))
    return wide + dot(hidden, down[...])


def near_rotated(spans, bases, slots, sources, out):
    @pl.loop(0, out.shape[0] // (2 * BALL))
    def _(step):
        for i in range(2):
            ball = 2 * step + i
            total = None
            for (block, start, rows), source in zip(spans, sources):
                at = slots[block][:, start : start + rows]
                part = picked_rows(at, source[...], ball * BALL + bases[0])
                total = part if total is None else total + part
            here = pl.ds(pl.multiple_of(ball * BALL, BALL), BALL)
            out[here, :] = total.astype(bf16)


def near_returned(spans, bases, wanted, sources, out):
    @pl.loop(0, out.shape[0] // (2 * BALL))
    def _(step):
        here = pl.ds(pl.multiple_of(step * 2 * BALL, 2 * BALL), 2 * BALL)
        want, total = wanted[here, :], None
        for (block, start, rows), source in zip(spans, sources):
            part = returned_rows(want, source[...], bases[block] + start)
            total = part if total is None else total + part
        out[here, :] = total.astype(bf16)


def last_first_kernel(before, spans, bases, slot_own, slot_core, slot_z, *refs):
    count = len(spans) - 1
    own, sources = refs[:5], refs[5 : 5 + count]
    out, near, held = refs[5 + count], refs[6 + count], refs[7 + count : 7 + 2 * count]
    sems = refs[7 + 2 * count]
    copies = [
        pltpu.make_async_copy(source, ref, sems.at[i])
        for i, (source, ref) in enumerate(zip(sources, held))
    ]
    first_kernel(before, *own, out, *refs[8 + 2 * count :], extra=copies)
    near_rotated(spans, bases, (slot_own, slot_core, slot_z), (*held, out), near)


def first_kernel(before, points, w_in, w_out, gate_up, down, *refs, extra=()):
    out, held, sems = refs[-7], refs[-6:-1], refs[-1]
    sources = (
        points.at[pl.ds(before * BALL, out.shape[0]), :],
        *(ref.at[pl.ds(0, 1)] for ref in (w_in, w_out, gate_up, down)),
    )
    copies = [
        pltpu.make_async_copy(source, ref, sems.at[i])
        for i, (source, ref) in enumerate(zip(sources, held))
    ]
    for copy in copies:
        copy.start()
    for copy in extra:
        copy.start()
    for copy in copies[:3]:
        copy.wait()
    rows, w_in, w_out, gate_up, down = held
    for pair in range(0, out.shape[0], 2 * BALL):
        mixed = []
        for at in range(pair, pair + 2 * BALL, BALL):
            wide = rows[at : at + BALL, :].astype(f32)
            mixed.append((wide + ball_attend(wide, w_in[0], w_out[0])).astype(bf16))
        if pair == 0:
            for copy in (*copies[3:], *extra):
                copy.wait()
        result = feed_forward(jnp.concatenate(mixed, 0), gate_up.at[0], down.at[0])
        out[pair : pair + 2 * BALL, :] = result.astype(bf16)


def picked_rows(slots, source, first_slot):
    want = lax.broadcasted_iota(jnp.int32, (BALL, 1), 0) + first_slot
    hot = jnp.where(want == slots, 1.0, 0.0).astype(bf16)
    return dot(hot, source)


def returned_rows(want, source, first_slot):
    hot = [
        jnp.where(want == first_slot + at, 1.0, 0.0).astype(bf16)
        for at in range(0, source.shape[0], LANES)
    ]
    return dot(jnp.concatenate(hot, 1), source)


def gather_rotated_kernel(spans, bases, *refs):
    count = len(spans)
    slots, sources, acc, out = refs[:4], refs[4 : 4 + count], refs[4 + count : -1], refs[-1]
    for i in range(2):
        here = slice(i * BALL, (i + 1) * BALL)
        first_slot = (2 * pl.program_id(0) + i) * BALL + bases[0]
        total = acc[0][here, :].astype(f32) if acc else None
        for (block, start, rows), source in zip(spans, sources):
            part = picked_rows(slots[block][:, start : start + rows], source[...], first_slot)
            total = part if total is None else total + part
        out[here, :] = total.astype(bf16)


def turn_kernel(spans, balls_before, bases, *refs):
    count = len(spans)
    slots, sources = refs[:4], refs[4 : 4 + count]
    acc, w_in, w_out = refs[4 + count : 7 + count]
    out = refs[-1]
    for i in range(acc.shape[0] // BALL):
        here = slice(i * BALL, (i + 1) * BALL)
        first_slot = (2 * pl.program_id(0) + i + balls_before) * BALL + bases[0]
        total = acc[here, :].astype(f32)
        for (block, start, rows), source in zip(spans, sources):
            total += picked_rows(slots[block][:, start : start + rows], source[...], first_slot)
        out[here, :] = ball_attend(total, w_in[0], w_out[0]).astype(bf16)


def last_turn_kernel(spans, near_spans, balls_before, bases, own_balls, *refs):
    count, held = len(spans), len(near_spans) - 1
    sources = refs[7 + count : 7 + count + held]
    out, near, wanted = refs[-3:]
    turn_kernel(spans, balls_before, bases, *refs[: 7 + count], out)
    for ball in range(own_balls.shape[0]):
        tall = jnp.broadcast_to(own_balls[ball].astype(f32), (LANES, BALL)).T
        lane = lax.broadcasted_iota(jnp.int32, (BALL, LANES), 1)
        wanted[ball * BALL : (ball + 1) * BALL, :] = tall.astype(jnp.int32) - lane
    near_returned(near_spans, bases, wanted, (*sources, out), near)


def gather_returned_kernel(spans, bases, wanted, *refs):
    count = len(spans)
    sources, acc, out = refs[:count], refs[count:-1], refs[-1]
    want = wanted[...]
    total = acc[0][...].astype(f32) if acc else None
    for (block, start, rows), source in zip(spans, sources):
        part = returned_rows(want, source[...], bases[block] + start)
        total = part if total is None else total + part
    out[...] = total.astype(bf16)


def second_kernel(spans, bases, wanted, *refs):
    count = len(spans)
    sources = refs[:count]
    acc, first_a, first_b, first_c, gate_up, down, pool_weight = refs[count : count + 7]
    second, pooled, pooled_normed = refs[count + 7 : -2]
    tall = refs[-2:]
    step = pl.program_id(0)
    want = wanted[...]
    returned = acc[...].astype(f32)
    for (block, start, rows), source in zip(spans, sources):
        returned += returned_rows(want, source[...], bases[block] + start)
    inner = jnp.where(step == 0, first_a[...], first_b[...])
    first = jnp.where(step == pl.num_programs(0) - 1, first_c[...], inner)
    mixed = (first.astype(f32) + returned).astype(bf16)
    result = feed_forward(mixed, gate_up.at[0], down.at[0]).astype(bf16)
    second[...] = result
    size = acc.shape[0]
    here = pl.ds(pl.multiple_of(step * size, size), size)
    for half, ref in enumerate(tall):
        ref[here, :] = result[:, half * LANES : (half + 1) * LANES].astype(f32)

    @pl.when(step == pl.num_programs(0) - 1)
    def _():
        width = result.shape[1]
        count = pooled.shape[0]
        total = None
        for j in range(CHILDREN):
            child = jnp.concatenate(
                [ref[pl.ds(j, count, stride=CHILDREN), :].astype(bf16) for ref in tall], 1
            )
            part = dot(child, pool_weight[j * width : (j + 1) * width, :])
            total = part if total is None else total + part
        rounded = total.astype(bf16)
        pooled[...] = rounded
        pooled_normed[...] = normed(rounded.astype(f32))


def coarse_share(queries, sources, w_in, keys, values):
    width = queries.shape[1]
    at = 0
    for source in sources:
        rows = source.shape[0]
        pair = dot(source[...], w_in[:, width:])
        keys[at : at + rows, :] = pair[:, :width].astype(bf16)
        values[at : at + rows, :] = pair[:, width:].astype(bf16)
        at += rows
    part = width // 2
    shares = []
    for half in range(2):
        cols = slice(half * part, (half + 1) * part)
        share = None
        for mask, query in masked_heads(queries[:, cols], CHEADS // 2):
            scores = lax.dot_general(query, keys[:at, cols], LANES_BOTH, preferred_element_type=f32)
            most = jnp.max(scores, axis=-1, keepdims=True)
            scores = jnp.exp2(scores - most)
            total = jnp.sum(scores, axis=-1, keepdims=True)
            mixed = dot(scores.astype(bf16), values[:at, cols])
            if share is None:
                share = [mixed] + [jnp.broadcast_to(x, mixed.shape) for x in (most, total)]
            else:
                share = [jnp.where(mask, x, old) for x, old in zip((mixed, most, total), share)]
        shares.append(share)
    return [jnp.concatenate(pair, 1) for pair in zip(*shares)]


def coarse_early_kernel(blocks, *refs):
    sources = refs[:blocks]
    w_in, out_queries, mixture, most, total, keys, values = refs[blocks:]
    width = out_queries.shape[1]
    scale = LOG2E / math.sqrt(width // CHEADS)
    queries = (dot(sources[0][...], w_in[:, :width]) * scale).astype(bf16)
    out_queries[...] = queries
    mixture[...], most[...], total[...] = coarse_share(queries, sources, w_in, keys, values)


def coarse_kernel(blocks, *refs):
    sources, early = refs[:blocks], refs[blocks : blocks + 4]
    pooled, second, w_in, w_out, gate_up, down, unpool, out, keys, values = refs[blocks + 4 : -2]
    tall = refs[-2:]
    mixed_late, most_late, total_late = coarse_share(early[0][...], sources, w_in, keys, values)
    mixed, most, total = (ref[...] for ref in early[1:])
    top = jnp.maximum(most, most_late)
    keep, keep_late = jnp.exp2(most - top), jnp.exp2(most_late - top)
    mixture = (mixed * keep + mixed_late * keep_late) / (total * keep + total_late * keep_late)
    stream = (pooled[...].astype(f32) + dot(mixture.astype(bf16), w_out[...])).astype(bf16)
    coarse = feed_forward(stream, gate_up, down).astype(bf16)
    source = normed(coarse.astype(f32))
    count, fine = source.shape[0], second.shape[1]
    for j in range(CHILDREN):
        lifted = dot(source, unpool[:, j * fine : (j + 1) * fine])
        for half, ref in enumerate(tall):
            lanes = slice(half * LANES, (half + 1) * LANES)
            ref[pl.ds(j, count, stride=CHILDREN), :] = lifted[:, lanes]
    for half, ref in enumerate(tall):
        lanes = slice(half * LANES, (half + 1) * LANES)
        out[:, lanes] = (second[:, lanes].astype(f32) + ref[...]).astype(bf16)


def whole(shape):
    return pl.BlockSpec(shape, lambda *_: (0,) * len(shape))


def layer(shape, index):
    return pl.BlockSpec((1,) + shape[1:], lambda *_: (index, 0, 0))


def ball_rows(width, before=0):
    return pl.BlockSpec((BALL, width), lambda i: (i + before, 0))


def params(mib=20):
    return pltpu.CompilerParams(vmem_limit_bytes=mib << 20)


def cost(gflop, mbyte):
    return pl.CostEstimate(
        flops=int(gflop * 1e9), bytes_accessed=int(mbyte * 1e6), transcendentals=0
    )


def swap(value, axis):
    return lax.ppermute(value, axis, [(0, 1), (1, 0)])


def turn_y(value, distance):
    size = lax.axis_size("y")
    return lax.ppermute(value, "y", [(i, (i + distance) % size) for i in range(size)])


def after(value, *others):
    if not others:
        return value
    return lax.optimization_barrier((value, *others))[0]


def spans_of(blocks, counts, wanted):
    spans, arrays = [], []
    for block, chunk in wanted:
        start = sum(counts[:chunk]) * BALL
        spans.append((block, start, counts[chunk] * BALL))
        arrays.append(blocks[block][chunk])
    return tuple(spans), arrays


def local(
    points,
    rotated_slot,
    fine_attend_in,
    fine_attend_out,
    fine_gate_up,
    fine_down,
    pool_weight,
    coarse_attend_in,
    coarse_attend_out,
    coarse_gate_up,
    coarse_down,
    unpool_weight,
):
    rows, width = points.shape
    balls = rows // BALL
    cols = lax.axis_size("x") * lax.axis_size("w") * lax.axis_size("y")
    mine = lax.axis_index("z") * 2 + lax.axis_index("c")
    col = lax.axis_index(("x", "w", "y"))

    own_slot = rotated_slot.reshape(1, rows)
    far_slot = lax.ppermute(own_slot, ("z", "c"), [(0, 3), (1, 2), (2, 1), (3, 0)])
    group_slots = [own_slot, swap(own_slot, "c"), swap(own_slot, "z"), far_slot]
    bases = jnp.stack([((mine ^ flip) * cols + col) * rows for flip in (0, 1, 2, 3)]).astype(
        jnp.int32
    )
    smem = pl.BlockSpec(memory_space=pltpu.SMEM)

    weights = (fine_attend_in, fine_attend_out, fine_gate_up, fine_down)
    first_chunks, arrived, before = [], [], 0
    hbm = pl.BlockSpec(memory_space=pl.ANY)
    smem = pl.BlockSpec(memory_space=pltpu.SMEM)
    vmem = pl.BlockSpec(memory_space=pltpu.VMEM)

    def scratch(count):
        return (
            [pltpu.VMEM((count * BALL, width), bf16)]
            + [pltpu.VMEM((1,) + weight.shape[1:], bf16) for weight in weights]
            + [pltpu.SemaphoreType.DMA((5,))]
        )

    for count in FIRST_CHUNKS[:-1]:
        pending = []
        if first_chunks:
            pending = [first_chunks[-1]] + group_slots[1:]
            arrived.append(swap(after(first_chunks[-1], *arrived[-1:]), "z"))
        first_chunks.append(
            pl.pallas_call(
                functools.partial(first_kernel, before),
                name="first",
                in_specs=[hbm] * 5,
                out_specs=vmem,
                out_shape=jax.ShapeDtypeStruct((count * BALL, width), bf16),
                scratch_shapes=scratch(count),
                compiler_params=params(60),
                cost_estimate=cost(1.2 * count, 0.5),
            )(after(points, *pending), *weights)
        )
        before += count
    last = len(FIRST_CHUNKS) - 1
    arrived.append(swap(after(first_chunks[-1], *arrived[-1:]), "z"))
    count = FIRST_CHUNKS[-1]
    siblings = [swap(first_chunks[0], "c")]
    blocks = [first_chunks, siblings, arrived, []]
    spans, arrays = spans_of(blocks, FIRST_CHUNKS, [(0, 0), (0, 1), (1, 0), (2, 0)])
    spans += ((0, before * BALL, count * BALL),)
    chunk, near = pl.pallas_call(
        functools.partial(last_first_kernel, before, spans),
        name="first_near",
        in_specs=[smem] + [vmem] * 3 + [hbm] * (5 + len(arrays)),
        out_specs=[vmem, vmem],
        out_shape=[
            jax.ShapeDtypeStruct((count * BALL, width), bf16),
            jax.ShapeDtypeStruct((rows, width), bf16),
        ],
        scratch_shapes=[pltpu.VMEM(array.shape, bf16) for array in arrays]
        + [pltpu.SemaphoreType.DMA((len(arrays),))]
        + scratch(count),
        compiler_params=params(60),
        cost_estimate=cost(6, 2),
    )(bases, *group_slots[:3], points, *weights, *arrays)
    first_chunks.append(chunk)
    arrived.append(swap(after(chunk, arrived[-1]), "z"))
    siblings += [swap(after(first_chunks[1], chunk), "c"), swap(chunk, "c")]
    blocks[3].extend(swap(block, "c") for block in arrived[:-1])
    own_balls = rotated_slot.reshape(balls, 1, BALL)
    two_balls = pl.BlockSpec((2 * BALL, width), lambda i: (i, 0))

    def gather_rotated(picked, acc):
        spans, arrays = spans_of(blocks, FIRST_CHUNKS, picked)
        return pl.pallas_call(
            functools.partial(gather_rotated_kernel, spans),
            name="gather_rotated",
            grid=(balls // 2,),
            in_specs=[smem]
            + [whole((1, rows))] * 4
            + [whole(array.shape) for array in arrays]
            + [two_balls] * len(acc),
            out_specs=two_balls,
            out_shape=jax.ShapeDtypeStruct((rows, width), bf16),
            compiler_params=params(),
            cost_estimate=cost(7, 4),
        )(bases, *group_slots, *arrays, *acc)

    rest = [(3, 0), (1, 1), (1, 2), (2, 1), (3, 1)]
    acc = gather_rotated(rest, [near])
    blocks[3].append(swap(after(blocks[2][last], acc), "c"))
    spans, arrays = spans_of(blocks, FIRST_CHUNKS, [(2, last), (3, last)])
    turned_chunks, arrived, before = [], [], 0
    for place, count in enumerate(TURN_CHUNKS):
        final = place == last
        kernel = functools.partial(turn_kernel, spans, before)
        extra, extra_specs = turned_chunks[-1:], [hbm] * len(turned_chunks[-1:])
        out_specs = [pl.BlockSpec((2 * BALL, width), lambda i: (i, 0))]
        out_shape = [jax.ShapeDtypeStruct((count * BALL, width), bf16)]
        columns, column_specs = [], []
        if final:
            siblings = [swap(turned_chunks[0], "c")]
            back = [turned_chunks, siblings, arrived, []]
            near_spans, extra = spans_of(back, TURN_CHUNKS, [(0, 0), (0, 1), (1, 0), (2, 0)])
            near_spans += ((0, before * BALL, count * BALL),)
            kernel = functools.partial(last_turn_kernel, spans, near_spans, before)
            extra_specs = [whole(array.shape) for array in extra]
            columns, column_specs = [own_balls], [whole(own_balls.shape)]
            out_specs += [whole((rows, width)), whole((rows, LANES))]
            out_shape += [
                jax.ShapeDtypeStruct((rows, width), bf16),
                jax.ShapeDtypeStruct((rows, LANES), jnp.int32),
            ]
        result = pl.pallas_call(
            kernel,
            name="turn_near" if final else "turn",
            grid=(count // 2,),
            in_specs=[smem]
            + column_specs
            + [whole((1, rows))] * 4
            + [whole(array.shape) for array in arrays]
            + [
                pl.BlockSpec((2 * BALL, width), lambda i, b=before // 2: (i + b, 0)),
                layer(fine_attend_in.shape, 1),
                layer(fine_attend_out.shape, 1),
            ]
            + extra_specs,
            out_specs=out_specs,
            out_shape=out_shape,
            compiler_params=params(),
            cost_estimate=cost(6 if final else 1.2 * count, 0.5),
        )(
            bases,
            *columns,
            *group_slots,
            *arrays,
            acc,
            fine_attend_in,
            fine_attend_out,
            *extra,
        )
        turned_chunks.append(result[0])
        arrived.append(swap(after(result[0], *arrived[-1:]), "z"))
        before += count
    near, wanted = result[1:]
    siblings += [swap(after(turned_chunks[1], result[0]), "c"), swap(result[0], "c")]
    back[3].extend(swap(block, "c") for block in arrived[:-1])
    last = len(TURN_CHUNKS) - 1

    def gather_returned(picked, acc):
        spans, arrays = spans_of(back, TURN_CHUNKS, picked)
        return pl.pallas_call(
            functools.partial(gather_returned_kernel, spans),
            name="gather_returned",
            grid=(balls // 2,),
            in_specs=[smem, pl.BlockSpec((2 * BALL, LANES), lambda i: (i, 0))]
            + [whole(array.shape) for array in arrays]
            + [two_balls] * len(acc),
            out_specs=two_balls,
            out_shape=jax.ShapeDtypeStruct((rows, width), bf16),
            compiler_params=params(),
            cost_estimate=cost(7, 4),
        )(bases, wanted, *arrays, *acc)

    acc = gather_returned(rest, [near])
    back[3].append(swap(after(back[2][last], acc), "c"))
    spans, arrays = spans_of(back, TURN_CHUNKS, [(2, last), (3, last)])
    pooled_rows, coarse_width = rows // CHILDREN, pool_weight.shape[1]
    second, pooled, pooled_normed = pl.pallas_call(
        functools.partial(second_kernel, spans),
        name="second",
        grid=(balls // 2,),
        in_specs=[smem, pl.BlockSpec((2 * BALL, LANES), lambda i: (i, 0))]
        + [whole(array.shape) for array in arrays]
        + [
            two_balls,
            pl.BlockSpec((2 * BALL, width), lambda i: (0, 0)),
            pl.BlockSpec((2 * BALL, width), lambda i: (jnp.clip(i - 1, 0, 1), 0)),
            pl.BlockSpec((2 * BALL, width), lambda i: (0, 0)),
            layer(fine_gate_up.shape, 1),
            layer(fine_down.shape, 1),
            whole(pool_weight.shape),
        ],
        out_specs=[
            two_balls,
            whole((pooled_rows, coarse_width)),
            whole((pooled_rows, coarse_width)),
        ],
        out_shape=[
            jax.ShapeDtypeStruct((rows, width), bf16),
            jax.ShapeDtypeStruct((pooled_rows, coarse_width), bf16),
            jax.ShapeDtypeStruct((pooled_rows, coarse_width), bf16),
        ],
        scratch_shapes=[pltpu.VMEM((rows, LANES), f32)] * 2,
        compiler_params=params(),
        cost_estimate=cost(8, 4),
    )(bases, wanted, *arrays, acc, *first_chunks, fine_gate_up, fine_down, pool_weight)

    other = swap(pooled_normed, "w")
    opposite = turn_y(pooled_normed, 2)
    up, down_y = turn_y(pooled_normed, 1), turn_y(pooled_normed, -1)
    late = [turn_y(other, 1), turn_y(other, -1), swap(opposite, "w")]
    soon = [pooled_normed, other, opposite, up, down_y]
    square = (pooled_rows, coarse_width)
    held = [pltpu.VMEM((pooled_rows * len(soon), coarse_width), bf16)] * 2
    early = pl.pallas_call(
        functools.partial(coarse_early_kernel, len(soon)),
        name="coarse_early",
        grid=(1,),
        in_specs=[whole(square)] * len(soon) + [whole(coarse_attend_in.shape)],
        out_specs=[whole(square)] * 4,
        out_shape=[jax.ShapeDtypeStruct(square, bf16)] + [jax.ShapeDtypeStruct(square, f32)] * 3,
        scratch_shapes=held,
        compiler_params=params(),
        cost_estimate=cost(5, 4),
    )(*soon, coarse_attend_in)
    operands = [
        *late,
        *early,
        pooled,
        second,
        coarse_attend_in,
        coarse_attend_out,
        coarse_gate_up,
        coarse_down,
        unpool_weight,
    ]
    return pl.pallas_call(
        functools.partial(coarse_kernel, len(late)),
        name="coarse",
        grid=(1,),
        in_specs=[whole(array.shape) for array in operands],
        out_specs=whole((rows, width)),
        out_shape=jax.ShapeDtypeStruct((rows, width), bf16),
        scratch_shapes=held + [pltpu.VMEM((rows, LANES), f32)] * 2,
        compiler_params=params(40),
        cost_estimate=cost(8, 16),
    )(*operands)


def solution(mesh):
    torus = Mesh(mesh.devices.reshape(2, 2, 4, 2, 4), AXES)
    split = P(AXES, None)
    return jax.shard_map(
        local,
        mesh=torus,
        in_specs=(split, P(AXES)) + (P(),) * 10,
        out_specs=split,
        check_vma=False,
    )
```
